256 devices in a mesh: seq: 32 (over y, z_lo, core), head: 8 (over x, z_hi).
Axes of the slice: x: 4, y: 4, z: 8 (z_hi: 2, z_lo: 4; z = z_hi * 4 + z_lo), core: 2. Of those that a mesh axis runs over, the one named last changes fastest.
Arguments:
- stream: bfloat16 [6144, 5120], P('seq', 'head'), may hold values from -57 to 57
- normed: bfloat16 [6144, 5120], P('seq', 'head'), may hold values from -41 to 41
- qkv_weight: bfloat16 [5120, 3, 3072], P(None, None, 'head'), may hold values from -0.078125 to 0.078125
- out_weight: bfloat16 [3072, 5120], P('head', 'seq'), may hold values from -0.109375 to 0.109375
- final_gain: float32 [5120], replicated, may hold values from 0.5 to 1.5
- final_weight: bfloat16 [5120, 64], P('seq'), may hold values from -0.078125 to 0.078125
- guide_stream: bfloat16 [6144, 2048], P('seq', 'head'), may hold values from -57 to 57
- guide_normed: bfloat16 [6144, 2048], P('seq', 'head'), may hold values from -41 to 41
- guide_qkv: bfloat16 [2048, 3, 1024], P('seq', None, 'head'), may hold values from -0.125 to 0.125
- guide_out: bfloat16 [1024, 2048], P('head', 'seq'), may hold values from -0.1875 to 0.1875
- guide_gain: float32 [2048], replicated, may hold values from 0.5 to 1.5
- guide_final: bfloat16 [2048, 64], P('seq'), may hold values from -0.125 to 0.125
- layout: int32 [6144], replicated, may hold values from 0 to 6143, each once
- flags: int32 [12], replicated, may hold values 0 or 1
Outputs:
- guided: float32 [6144, 64], P('seq')
The draws below stay inside these ranges and needn't reach their ends.
Inputs may be any that keep to these rules, and one draw needn't show every extreme that they name: `layout`: each token appears in exactly one slot.
All inputs are finite; a program needn't handle non-finite values.
Results may differ from the reference program's by a relative error of at most 0.02.
The reference program's roundings to bfloat16 on the way count: a program that leaves them out, or rounds other values in their place, can miss the bound.
Values may be sent and summed in bfloat16 or wider, within the bound.
A program may use at most 128 MiB of HBM per device.

```python
import math
import jax
import jax.numpy as jnp
from jax import lax

D = 5120
HD = 128
HEADS = 24
GD = 2048
GHEADS = 8
P_SIZE = 64
TOKENS = 6144
FRAME_TOK = 512
FRAMES = 12


def draw_stream(key, part):
    key = jax.random.fold_in(key, 11)
    return jnp.clip(jax.random.normal(key, (TOKENS, D), jnp.float32), -4.0, 4.0).astype(jnp.bfloat16)


def draw_normed(key, part):
    key = jax.random.fold_in(key, 12)
    return jnp.clip(jax.random.normal(key, (TOKENS, D), jnp.float32), -4.0, 4.0).astype(jnp.bfloat16)


def draw_guide_stream(key, part):
    key = jax.random.fold_in(key, 13)
    return jnp.clip(jax.random.normal(key, (TOKENS, GD), jnp.float32), -4.0, 4.0).astype(jnp.bfloat16)


def draw_guide_normed(key, part):
    key = jax.random.fold_in(key, 14)
    return jnp.clip(jax.random.normal(key, (TOKENS, GD), jnp.float32), -4.0, 4.0).astype(jnp.bfloat16)


def place_ends(entries, own_key, least, top_value):
    longest = entries.shape.index(max(entries.shape))
    spots = []
    for shift in (0, 1):
        where = [jax.random.randint(jax.random.fold_in(own_key, axis), (), 0, length) for axis, length in enumerate(entries.shape)]
        where[longest] = (where[longest] + shift) % entries.shape[longest]
        spots.append(tuple(where))
    return entries.at[spots[0]].set(least).at[spots[1]].set(top_value)


def level_of(own_key, dims, cuts, smallest, largest):
    loudness, own = 1.0, jax.random.fold_in(own_key, 6)
    for axis_at, blocks in cuts:
        steps = jnp.exp(jax.random.uniform(jax.random.fold_in(own, axis_at), (blocks,), jnp.float32, smallest / len(cuts), largest / len(cuts)))
        loudness = loudness * jnp.repeat(steps, dims[axis_at] // blocks).reshape([-1 if axis == axis_at else 1 for axis in range(len(dims))])
    return loudness


def bell_draw(rng, dims, scale, most, shards=(), held_as=jnp.bfloat16):
    entries = jax.random.normal(rng, dims, jnp.float32) * scale
    if len(shards) > 0:
        entries = level_of(rng, dims, shards, -0.22, 0.18) * entries
    return jnp.clip(entries, min=-most, max=most).astype(held_as)


def setup_inputs(seed: int = 0) -> dict:
    splits = jax.random.split(jax.random.key(seed), 15)
    return {
        "stream": draw_stream(jax.random.fold_in(splits[14], 71), 0),
        "normed": draw_normed(jax.random.fold_in(splits[14], 71), 0),
        "qkv_weight": bell_draw(splits[2], (D, 3, HEADS * HD), D ** -0.5, 0.078125, ((2, 8),)),
        "out_weight": bell_draw(splits[3], (HEADS * HD, D), (HEADS * HD) ** -0.5, 0.109375, ((0, 8), (1, 32))),
        "final_gain": jnp.clip(1.0 + 0.1 * jax.random.normal(splits[4], (D,), jnp.float32), 0.5, 1.5),
        "final_weight": bell_draw(splits[5], (D, P_SIZE), D ** -0.5, 0.078125, ((0, 32),)),
        "guide_stream": draw_guide_stream(jax.random.fold_in(splits[14], 71), 0),
        "guide_normed": draw_guide_normed(jax.random.fold_in(splits[14], 71), 0),
        "guide_qkv": bell_draw(splits[8], (GD, 3, GHEADS * HD), GD ** -0.5, 0.125, ((0, 32), (2, 8))),
        "guide_out": bell_draw(splits[9], (GHEADS * HD, GD), (GHEADS * HD) ** -0.5, 0.1875, ((0, 8), (1, 32))),
        "guide_gain": jnp.clip(1.0 + 0.1 * jax.random.normal(splits[10], (GD,), jnp.float32), 0.5, 1.5),
        "guide_final": bell_draw(splits[11], (GD, P_SIZE), GD ** -0.5, 0.125, ((0, 32),)),
        "layout": jax.random.permutation(splits[12], TOKENS).astype(jnp.int32),
        "flags": place_ends((jax.random.randint(splits[13], (FRAMES,), 0, 4) < 3).astype(jnp.int32), jax.random.fold_in(splits[13], 1), 0, 1),
    }


EPS = 1e-05
TEMPER = 2.5

def attend_head(queries, keys, values):
    row_count = queries.shape[0]
    block_rows = min(512, row_count)
    factor = TEMPER / math.sqrt(queries.shape[1])

    def one_block(block):
        scores = jnp.dot(block, keys.T, preferred_element_type=jnp.float32) * factor
        highest = lax.optimization_barrier(jnp.max(scores, axis=1, keepdims=True))
        expd = jnp.exp(scores - highest)
        totals = lax.optimization_barrier(jnp.sum(expd, axis=1, keepdims=True))
        mixed = jnp.dot(expd.astype(jnp.bfloat16), values, preferred_element_type=jnp.float32)
        return (mixed / totals).astype(jnp.bfloat16)
    blocks = queries.reshape(row_count // block_rows, block_rows, queries.shape[1])
    return lax.map(one_block, blocks).reshape(row_count, queries.shape[1])

def layer_norm(hidden, gains):
    center = lax.optimization_barrier(jnp.mean(hidden, axis=1, keepdims=True))
    square = lax.optimization_barrier(jnp.mean(hidden * hidden, axis=1, keepdims=True))
    spread = square - center * center
    return ((hidden - center) * lax.rsqrt(spread + EPS) * gains.astype(jnp.float32)).astype(jnp.bfloat16)

def model_pred(residual, attn_input, qkv_w, out_w, gains, final_w):
    row_count, width = attn_input.shape
    head_count = qkv_w.shape[2] // HD
    packed = jnp.dot(attn_input, qkv_w.reshape(width, 3 * head_count * HD), preferred_element_type=jnp.float32)
    packed = packed.astype(jnp.bfloat16).reshape(row_count, 3, head_count, HD)
    triple = jnp.transpose(packed, (1, 2, 0, 3))

    def per_head(group):
        return attend_head(group[0], group[1], group[2])
    attended = lax.map(per_head, (triple[0], triple[1], triple[2]))
    attended = jnp.transpose(attended, (1, 0, 2)).reshape(row_count, head_count * HD)
    hidden = residual.astype(jnp.float32) + jnp.dot(attended, out_w, preferred_element_type=jnp.float32)
    normal = layer_norm(hidden, gains)
    return jnp.dot(normal, final_w, preferred_element_type=jnp.float32)

def reference(stream, normed, qkv_weight, out_weight, final_gain, final_weight, guide_stream, guide_normed, guide_qkv, guide_out, guide_gain, guide_final, layout, flags):
    main_pred = model_pred(stream, normed, qkv_weight, out_weight, final_gain, final_weight)
    slot_pred = model_pred(guide_stream, guide_normed, guide_qkv, guide_out, guide_gain, guide_final)
    guide_pred = jnp.zeros_like(slot_pred).at[layout].set(slot_pred)
    frame_ids = jnp.arange(TOKENS, dtype=jnp.int32) // FRAME_TOK
    strength = 1.0 + flags[frame_ids].astype(jnp.float32)
    return guide_pred + strength[:, None] * (main_pred - guide_pred)
```

```python
import math

import jax
import jax.numpy as jnp
from jax import lax
from jax.experimental import pallas as pl
from jax.experimental.pallas import tpu as pltpu
from jax.sharding import PartitionSpec as P

HD = 128
FRAME_TOK = 512
EPS = 1e-05
TEMPER = 2.5
SCALE2 = TEMPER / math.sqrt(HD) * math.log2(math.e)
F32, BF16 = jnp.float32, jnp.bfloat16
MESH = pl.DeviceIdType.MESH

ROWS = 192
HALF = 96
KC, GKC = 640, 256
TOKENS = 6144
QT = 256
NT = (((1,), (1,)), ((), ()))
TN = (((0,), (0,)), ((), ()))


def body(
    stream, normed, qkv_t, out_t, gain, fin, gstream, gnormed, gqkv_t, gout_t, ggain, gfin,
    layout, flags, out,
    xn, gn, qw, gq, wt, gwt, fw, gfw, sb, gsb, acc, gacc, packed, qb, kv, top, tot, ot, ob, at,
    hot, hid, ghid, sg, sm, pg, pm, rg, rm, gp, outb,
    send_sem, recv_sem, local_sem,
):
    s, g = lax.axis_index("seq"), lax.axis_index("head")
    y, zl, c = s // 8, (s // 2) % 4, s % 2
    x, zh = g // 2, g % 2

    def seq_of(yy, zz, cc):
        return yy * 8 + zz * 2 + cc

    def head_of(xx, hh):
        return xx * 2 + hh

    xp, xm, x2 = (x + 1) % 4, (x + 3) % 4, (x + 2) % 4
    yp, ym, y2 = (y + 1) % 4, (y + 3) % 4, (y + 2) % 4
    oc, oh = 1 - c, 1 - zh
    started = []
    count = [0]

    def role():
        count[0] += 1
        return count[0] - 1

    def copy(r, src, dst, ss, gg):
        return pltpu.make_async_remote_copy(
            src_ref=src, dst_ref=dst, send_sem=send_sem.at[r], recv_sem=recv_sem.at[r],
            device_id=(ss, gg), device_id_type=MESH,
        )

    def send(r, src, dst, ss, gg):
        one = copy(r, src, dst, ss, gg)
        one.start()
        started.append(one)

    def wait(r, dst):
        copy(r, dst, dst, seq_of(y, zl, oc), g).wait_recv()

    part_s, part_g = g * 4 + s % 4, s // 4
    same = jnp.logical_and(x == y, zh == zl // 2)
    barrier = pltpu.get_barrier_semaphore()
    peers = [(seq_of(y, (zl + d) % 4, c), g) for d in (1, 2, 3)]
    peers += [(seq_of(y, (zl + d) % 4, c), head_of(x, oh)) for d in (0, 1, 2, 3)]
    peers += [(s, head_of((x + d) % 4, h)) for d in (1, 2, 3) for h in (zh, oh)]
    peers += [(seq_of((y + d) % 4, zl, c), g) for d in (1, 2, 3)]
    peers += [(seq_of(y, zl, oc), g)]
    for ss, gg in peers:
        pl.semaphore_signal(barrier, inc=1, device_id=(ss, gg), device_id_type=MESH)

    @pl.when(jnp.logical_not(same))
    def _():
        pl.semaphore_signal(barrier, inc=1, device_id=(part_s, part_g), device_id_type=MESH)

    local = [
        (normed, xn.at[g]), (gnormed, gn.at[g]), (gqkv_t, gq.at[:, y, zl, c]),
        (qkv_t, qw), (stream, sb), (gstream, gsb),
    ]
    local = [pltpu.make_async_copy(a, b, local_sem.at[i]) for i, (a, b) in enumerate(local)]
    for one in local:
        one.start()

    pl.semaphore_wait(barrier, len(peers) + 1 - same.astype(jnp.int32))

    sets = [(xn, normed), (gn, gnormed)]
    r_cross = [role(), role()]
    r_p, r_m = [[role(), role()] for _ in sets], [[role(), role()] for _ in sets]
    r_rp, r_rm = [[role(), role()] for _ in sets], [[role(), role()] for _ in sets]
    for i, (buf, src) in enumerate(sets):
        send(r_cross[i], src, buf.at[g], s, head_of(x, oh))
    for i, (buf, src) in enumerate(sets):
        send(r_p[i][0], src, buf.at[g], s, head_of(xp, zh))
        send(r_m[i][0], src, buf.at[g], s, head_of(xm, zh))
    r_gqz = [role() for _ in range(3)]
    for d in (1, 2, 3):
        send(r_gqz[d - 1], gqkv_t, gq.at[:, y, zl, c], seq_of(y, (zl + d) % 4, c), g)

    moved = [
        (out_t, wt.at[x, zh * 2 + zl % 2, c], wt.at[y, zl, c]),
        (gout_t, gwt.at[x, zh * 2 + zl % 2, c], gwt.at[y, zl, c]),
        (fin, fw.at[zl % 2, c], fw.at[zl % 2, c]),
        (gfin, gfw.at[zl % 2, c], gfw.at[zl % 2, c]),
    ]
    r_perm = [role() for _ in moved]

    @pl.when(jnp.logical_not(same))
    def _():
        for r, (src, there, _) in zip(r_perm, moved):
            copy(r, src, there, part_s, part_g).start()

    @pl.when(same)
    def _():
        for r, (src, _, here) in zip(r_perm, moved):
            pltpu.make_async_copy(src, here, recv_sem.at[r]).start()

    token = s * ROWS + lax.broadcasted_iota(jnp.int32, (ROWS, 128), 0)
    for r in range(TOKENS // 128):
        row = layout[pl.ds(r, 1), :]
        hot[:, r * 128 : (r + 1) * 128] = jnp.where(token == row, 1.0, 0.0).astype(BF16)

    def relay(i, h):
        buf = sets[i][0]
        k = 0 if h is zh else 1
        from_m, from_p = head_of(xm, h), head_of(xp, h)
        wait(r_p[i][k], buf.at[from_m])
        send(r_rp[i][k], buf.at[from_m, 0:HALF], buf.at[from_m, 0:HALF], s, head_of(xp, zh))
        wait(r_m[i][k], buf.at[from_p])
        send(r_rm[i][k], buf.at[from_p, HALF:], buf.at[from_p, HALF:], s, head_of(xm, zh))

    def far(i, h):
        buf = sets[i][0]
        k = 0 if h is zh else 1
        wait(r_rp[i][k], buf.at[head_of(x2, h), 0:HALF])
        wait(r_rm[i][k], buf.at[head_of(x2, h), HALF:])

    def project(gg, first=False):
        rows = xn[gg]
        for i in range(3):
            part = jnp.dot(
                rows, qw[i, pl.ds(pl.multiple_of(gg * KC, KC), KC), :], preferred_element_type=F32
            )
            acc[i] = part if first else acc[i] + part

    def gproject(gg, first=False):
        rows = gn[gg]
        for i in range(3):
            block = gq[i, gg // 2, pl.ds((gg % 2) * 2, 2)].reshape(GKC, HD)
            part = jnp.dot(rows, block, preferred_element_type=F32)
            gacc[i] = part if first else gacc[i] + part

    relay(0, zh)
    relay(1, zh)
    for i, (buf, _) in enumerate(sets):
        other = buf.at[head_of(x, oh)]
        wait(r_cross[i], other)
        send(r_p[i][1], other, other, s, head_of(xp, zh))
        send(r_m[i][1], other, other, s, head_of(xm, zh))
    local[2].wait()
    for d in (1, 2, 3):
        wait(r_gqz[d - 1], gq.at[:, y, (zl + 4 - d) % 4, c])
    r_gqp, r_gqm, r_gqrp, r_gqrm, r_gqc = role(), role(), role(), role(), role()
    mine = gq.at[:, y, :, c]
    send(r_gqp, mine, mine, seq_of(yp, zl, c), g)
    send(r_gqm, mine, mine, seq_of(ym, zl, c), g)
    for r, (_, _, here) in zip(r_perm, moved):
        wait(r, here)
    r_wz, r_gwz = [role() for _ in range(3)], [role() for _ in range(3)]
    for d in (1, 2, 3):
        there = seq_of(y, (zl + d) % 4, c)
        send(r_wz[d - 1], wt.at[y, zl, c], wt.at[y, zl, c], there, g)
        send(r_gwz[d - 1], gwt.at[y, zl, c], gwt.at[y, zl, c], there, g)
    zn = zl + 1 - 2 * (zl % 2)
    r_fz, r_gfz = role(), role()
    send(r_fz, fw.at[zl % 2, c], fw.at[zl % 2, c], seq_of(y, zn, c), g)
    send(r_gfz, gfw.at[zl % 2, c], gfw.at[zl % 2, c], seq_of(y, zn, c), g)

    for i in (0, 1, 3):
        local[i].wait()
    project(g, True)
    project(head_of(xm, zh))
    project(head_of(xp, zh))
    a, b = gq.at[:, ym, 0:2, c], gq.at[:, yp, 2:4, c]
    wait(r_gqp, gq.at[:, ym, :, c])
    send(r_gqrp, a, a, seq_of(yp, zl, c), g)
    wait(r_gqm, gq.at[:, yp, :, c])
    send(r_gqrm, b, b, seq_of(ym, zl, c), g)
    project(head_of(x, oh))
    relay(0, oh)
    relay(1, oh)
    far(0, zh)
    project(head_of(x2, zh))
    wait(r_gqrp, gq.at[:, y2, 0:2, c])
    wait(r_gqrm, gq.at[:, y2, 2:4, c])
    send(r_gqc, gq.at[:, :, :, c], gq.at[:, :, :, c], seq_of(y, zl, oc), g)
    project(head_of(xm, oh))
    project(head_of(xp, oh))
    wait(r_gqc, gq.at[:, :, :, oc])
    far(1, zh)
    gproject(g, True)
    for gg in (head_of(xm, zh), head_of(xp, zh), head_of(x2, zh), head_of(x, oh)):
        gproject(gg)
    gproject(head_of(xm, oh))
    gproject(head_of(xp, oh))
    far(0, oh)
    project(head_of(x2, oh))
    far(1, oh)
    gproject(head_of(x2, oh))
    for i in range(3):
        for j in range(3):
            packed[i, j] = acc[i, :, j * HD : (j + 1) * HD].astype(BF16)
        packed[i, 3] = gacc[i].astype(BF16)

    own = [
        pltpu.make_async_copy(packed.at[0, zl], qb.at[zl], local_sem.at[6]),
        pltpu.make_async_copy(packed.at[1:3, zl], kv.at[:, y, c, zl], local_sem.at[7]),
    ]
    for one in own:
        one.start()
    r_q, r_kv = [role() for _ in range(3)], [role() for _ in range(3)]
    for d in (1, 2, 3):
        j = (zl + d) % 4
        there = seq_of(y, j, c)
        send(r_kv[d - 1], packed.at[1:3, j], kv.at[:, y, c, zl], there, g)
    for d in (1, 2, 3):
        j = (zl + d) % 4
        send(r_q[d - 1], packed.at[0, j], qb.at[zl], seq_of(y, j, c), g)
    r_kp, r_km = [role() for _ in range(4)], [role() for _ in range(4)]
    r_kc, r_kr = [role() for _ in range(4)], [role() for _ in range(4)]
    r_kcm, r_kcp, r_kc2 = role(), role(), role()
    for d in range(4):
        k = (zl + 4 - d) % 4
        block = kv.at[:, y, c, k]
        if d == 0:
            own[1].wait()
        else:
            wait(r_kv[d - 1], block)
        send(r_kp[d], block, block, seq_of(yp, zl, c), g)
        send(r_km[d], block, block, seq_of(ym, zl, c), g)
        send(r_kc[d], block, block, seq_of(y, zl, oc), g)
    own[0].wait()
    for d in (1, 2, 3):
        wait(r_q[d - 1], qb.at[(zl + 4 - d) % 4])

    def absorb(yy, cc, first=False):
        keys = kv[0, yy, cc].reshape(4 * ROWS, HD)
        values = kv[1, yy, cc].reshape(4 * ROWS, HD)

        def tile(t, _):
            scores = lax.dot_general(
                keys, ob[pl.ds(pl.multiple_of(t * QT, QT), QT), :], NT, preferred_element_type=F32
            )
            highest = jnp.max(scores, axis=0, keepdims=True)
            if not first:
                before = top[t]
                highest = jnp.maximum(highest, before)
            expd = jnp.exp2((scores - highest) * SCALE2)
            total = jnp.sum(expd, axis=0, keepdims=True)
            mixed = lax.dot_general(values, expd.astype(BF16), TN, preferred_element_type=F32)
            top[t] = highest
            if first:
                tot[t] = total
                ot[t] = mixed
            else:
                shrink = jnp.exp2((before - highest) * SCALE2)
                tot[t] = tot[t] * shrink + total
                ot[t] = ot[t] * shrink + mixed
            return 0

        lax.fori_loop(0, 3, tile, 0)

    for k in range(4):
        ob[k * ROWS : (k + 1) * ROWS, :] = qb[k]
    absorb(y, c, True)
    for d in (0, 1):
        k = (zl + 4 - d) % 4
        wait(r_kp[d], kv.at[:, ym, c, k])
        send(r_kr[d], kv.at[:, ym, c, k], kv.at[:, ym, c, k], seq_of(yp, zl, c), g)
    for d in (2, 3):
        k = (zl + 4 - d) % 4
        wait(r_km[d], kv.at[:, yp, c, k])
        send(r_kr[d], kv.at[:, yp, c, k], kv.at[:, yp, c, k], seq_of(ym, zl, c), g)
    for d in range(4):
        wait(r_kc[d], kv.at[:, y, oc, (zl + 4 - d) % 4])
    absorb(y, oc)
    for d in (2, 3):
        wait(r_kp[d], kv.at[:, ym, c, (zl + 4 - d) % 4])
    send(r_kcm, kv.at[:, ym, c], kv.at[:, ym, c], seq_of(y, zl, oc), g)
    for d in (0, 1):
        wait(r_km[d], kv.at[:, yp, c, (zl + 4 - d) % 4])
    send(r_kcp, kv.at[:, yp, c], kv.at[:, yp, c], seq_of(y, zl, oc), g)
    for d in (1, 2, 3):
        wait(r_wz[d - 1], wt.at[y, (zl + 4 - d) % 4, c])
        wait(r_gwz[d - 1], gwt.at[y, (zl + 4 - d) % 4, c])
    r_w = [[role() for _ in range(6)] for _ in range(2)]
    for r, buf in zip(r_w, (wt, gwt)):
        block = buf.at[y, :, c]
        send(r[0], block, block, seq_of(yp, zl, c), g)
        send(r[1], block, block, seq_of(ym, zl, c), g)
    wait(r_fz, fw.at[1 - zl % 2, c])
    wait(r_gfz, gfw.at[1 - zl % 2, c])
    r_fc, r_gfc = role(), role()
    send(r_fc, fw.at[:, c], fw.at[:, c], seq_of(y, zl, oc), g)
    send(r_gfc, gfw.at[:, c], gfw.at[:, c], seq_of(y, zl, oc), g)
    absorb(ym, c)
    absorb(yp, c)
    for d in range(4):
        wait(r_kr[d], kv.at[:, y2, c, (zl + 4 - d) % 4])
    send(r_kc2, kv.at[:, y2, c], kv.at[:, y2, c], seq_of(y, zl, oc), g)
    wait(r_kcm, kv.at[:, ym, oc])
    absorb(ym, oc)
    wait(r_kcp, kv.at[:, yp, oc])
    absorb(yp, oc)
    absorb(y2, c)
    for r, buf in zip(r_w, (wt, gwt)):
        a, b = buf.at[ym, 0:2, c], buf.at[yp, 2:4, c]
        wait(r[0], buf.at[ym, :, c])
        send(r[2], a, a, seq_of(yp, zl, c), g)
        wait(r[1], buf.at[yp, :, c])
        send(r[3], b, b, seq_of(ym, zl, c), g)
    wait(r_kc2, kv.at[:, y2, oc])
    absorb(y2, oc)
    for t in range(3):
        done = (ot[t] / tot[t]).T.astype(BF16)
        ob[t * QT : (t + 1) * QT, :] = done

    r_o = [[role(), role()] for _ in range(4)]
    for d in (0, 1, 2, 3):
        k = (zl + d) % 4
        block = ob.at[pl.ds(pl.multiple_of(k * ROWS, ROWS), ROWS), :]
        for e, h in enumerate((zh, oh)):
            if d == 0 and e == 0:
                pltpu.make_async_copy(block, at.at[x, zh, zl], recv_sem.at[r_o[0][0]]).start()
            else:
                send(r_o[d][e], block, at.at[x, zh, zl], seq_of(y, k, c), head_of(x, h))
    first_o = r_o[0][0]

    def arrived(j):
        d = (zl + 4 - j) % 4
        for e, h in enumerate((zh, oh)):
            wait(first_o + d * 2 + e, at.at[x, h, j])

    r_gx = [role() for _ in range(4)]
    r_mx = [role() for _ in range(4)]
    arrived(3)
    send(r_gx[0], at.at[x, :, 3], at.at[x, :, 3], s, head_of(xp, zh))
    send(r_gx[1], at.at[x, :, 3], at.at[x, :, 3], s, head_of(xm, zh))
    for j in range(3):
        arrived(j)
    send(r_mx[0], at.at[x, :, 0:3], at.at[x, :, 0:3], s, head_of(xp, zh))
    send(r_mx[1], at.at[x, :, 0:3], at.at[x, :, 0:3], s, head_of(xm, zh))

    for r, buf in zip(r_w, (wt, gwt)):
        wait(r[2], buf.at[y2, 0:2, c])
        wait(r[3], buf.at[y2, 2:4, c])
        send(r[4], buf.at[:, :, c], buf.at[:, :, c], seq_of(y, zl, oc), g)
    wait(r_gx[0], at.at[xm, :, 3])
    send(r_gx[2], at.at[xm, 0, 3], at.at[xm, 0, 3], s, head_of(xp, zh))
    wait(r_gx[1], at.at[xp, :, 3])
    send(r_gx[3], at.at[xp, 1, 3], at.at[xp, 1, 3], s, head_of(xm, zh))
    local[4].wait()
    local[5].wait()
    wait(r_w[1][4], gwt.at[:, :, oc])

    def gout_part(xx):
        total = None
        for h in range(2):
            block = gwt[xx, h * 2 : h * 2 + 2].reshape(GKC, HD)
            part = lax.dot_general(at[xx, h, 3], block, NT, preferred_element_type=F32)
            total = part if total is None else total + part
        return total

    def out_part(xx):
        total = None
        for h in range(2):
            rows = jnp.concatenate([at[xx, h, j] for j in range(3)], axis=1)
            block = wt[xx, h * 2 : h * 2 + 2].reshape(KC, 3 * HD)
            part = lax.dot_general(rows, block, NT, preferred_element_type=F32)
            total = part if total is None else total + part
        return total

    ghid[...] = gsb[...].astype(F32) + gout_part(x)
    ghid[...] += gout_part(xm)
    ghid[...] += gout_part(xp)
    wait(r_w[0][4], wt.at[:, :, oc])
    hid[...] = sb[...].astype(F32) + out_part(x)
    wait(r_mx[0], at.at[xm, :, 0:3])
    send(r_mx[2], at.at[xm, 0, 0:3], at.at[xm, 0, 0:3], s, head_of(xp, zh))
    wait(r_mx[1], at.at[xp, :, 0:3])
    send(r_mx[3], at.at[xp, 1, 0:3], at.at[xp, 1, 0:3], s, head_of(xm, zh))
    wait(r_gx[2], at.at[x2, 0, 3])
    wait(r_gx[3], at.at[x2, 1, 3])
    ghid[...] += gout_part(x2)

    def spread_stats(buf, ref, width, roles):
        one = jnp.zeros((ROWS, 128), F32)
        two = jnp.zeros((ROWS, 128), F32)
        for i in range(width // 128):
            cols = ref[:, i * 128 : (i + 1) * 128]
            one = one + cols
            two = two + cols * cols
        buf[g, 0:1, :] = jnp.sum(one.T, axis=0, keepdims=True)
        buf[g, 1:2, :] = jnp.sum(two.T, axis=0, keepdims=True)
        buf[g, 2:8, :] = jnp.zeros((6, ROWS), F32)
        for d in range(1, 8):
            send(roles[d - 1], buf.at[g], buf.at[g], s, (g + d) % 8)

    def gather_stats(buf, width, roles):
        for d in range(1, 8):
            wait(roles[d - 1], buf.at[(g + 8 - d) % 8])
        sums = buf[0]
        for i in range(1, 8):
            sums = sums + buf[i]
        sums = sums * (1.0 / width)
        center = sums[0:1]
        scale = lax.rsqrt(sums[1:2] - center * center + EPS)
        return jnp.broadcast_to(center, (128, ROWS)).T, jnp.broadcast_to(scale, (128, ROWS)).T

    def predict(ref, width, center, scale, gains, weights):
        parts = []
        for i in range(width // 128):
            row = gains[pl.ds(g * (width // 128) + i, 1), :]
            cols = ref[:, i * 128 : (i + 1) * 128]
            parts.append(((cols - center) * scale * row).astype(BF16))
        normal = jnp.concatenate(parts, axis=1)
        return jnp.dot(normal, weights[...].reshape(width, 64), preferred_element_type=F32).T

    def spread_pred(pred, keep, buf, roles):
        for i in range(8):
            keep[i] = pred[i * 8 : (i + 1) * 8]
        for d in range(1, 8):
            k = (g + d) % 8
            send(roles[d - 1], keep.at[k], buf.at[g], s, k)
        buf[g] = keep[g]

    def gather_pred(buf, roles):
        for d in range(1, 8):
            wait(roles[d - 1], buf.at[(g + 8 - d) % 8])
        total = buf[0]
        for i in range(1, 8):
            total = total + buf[i]
        return total

    r_sg, r_sm, r_pg, r_pm, r_out = ([role() for _ in range(7)] for _ in range(5))
    spread_stats(sg, ghid, GKC, r_sg)
    hid[...] += out_part(xm)
    wait(r_fc, fw.at[:, oc])
    wait(r_gfc, gfw.at[:, oc])
    center, scale = gather_stats(sg, 2048, r_sg)
    spread_pred(predict(ghid, GKC, center, scale, ggain, gfw), pg, rg, r_pg)
    hid[...] += out_part(xp)
    gp[y, zl, c] = gather_pred(rg, r_pg)
    r_az, r_ay, r_ac = [role() for _ in range(3)], [role() for _ in range(3)], role()
    for d in (1, 2, 3):
        block = gp.at[y, zl, c]
        send(r_az[d - 1], block, block, seq_of(y, (zl + d) % 4, c), g)
    wait(r_mx[2], at.at[x2, 0, 0:3])
    wait(r_mx[3], at.at[x2, 1, 0:3])
    hid[...] += out_part(x2)
    spread_stats(sm, hid, KC, r_sm)
    for d in (1, 2, 3):
        wait(r_az[d - 1], gp.at[y, (zl + 4 - d) % 4, c])
    for d in (1, 2, 3):
        block = gp.at[y, :, c]
        send(r_ay[d - 1], block, block, seq_of((y + d) % 4, zl, c), g)
    center, scale = gather_stats(sm, 5120, r_sm)
    spread_pred(predict(hid, KC, center, scale, gain, fw), pm, rm, r_pm)
    for d in (1, 2, 3):
        wait(r_ay[d - 1], gp.at[(y + 4 - d) % 4, :, c])
    block = gp.at[:, :, c]
    send(r_ac, block, block, seq_of(y, zl, oc), g)
    wait(r_ac, gp.at[:, :, oc])

    lane = lax.broadcasted_iota(jnp.int32, (8, 128), 1)
    pieces = []
    for yy in range(4):
        for zz in range(4):
            a0, a1 = gp[yy, zz, 0, :, 0:128], gp[yy, zz, 0, :, 128:192]
            b0, b1 = gp[yy, zz, 1, :, 0:64], gp[yy, zz, 1, :, 64:192]
            pieces += [a0, jnp.concatenate([a1, b0], axis=1), b1]
    slots = jnp.concatenate(pieces, axis=1)
    high = slots.astype(BF16)
    low = (slots - high.astype(F32)).astype(BF16)
    picked = lax.dot_general(high, hot[...], NT, preferred_element_type=F32)
    picked = picked + lax.dot_general(low, hot[...], NT, preferred_element_type=F32)

    first = s * ROWS
    frame = first // FRAME_TOK
    last = (first + ROWS - 1) // FRAME_TOK
    owned = first + lax.broadcasted_iota(jnp.int32, (8, ROWS), 1)
    strength = 1.0 + jnp.where(owned // FRAME_TOK == frame, flags[frame], flags[last]).astype(F32)
    outb[g] = picked + strength * (gather_pred(rm, r_pm) - picked)
    for d in range(1, 8):
        send(r_out[d - 1], outb.at[g], outb.at[g], s, (g + d) % 8)
    for d in range(1, 8):
        wait(r_out[d - 1], outb.at[(g + 8 - d) % 8])
    for i in range(8):
        out[i * 8 : (i + 1) * 8, :] = outb[i]

    for one in started:
        one.wait_send()

    @pl.when(jnp.logical_not(same))
    def _():
        for r, (src, there, _) in zip(r_perm, moved):
            copy(r, src, there, part_s, part_g).wait_send()


def per_device(
    stream, normed, qkv_weight, out_weight, final_gain, final_weight, guide_stream, guide_normed,
    guide_qkv, guide_out, guide_gain, guide_final, layout, flags,
):
    anyw = pl.BlockSpec(memory_space=pl.ANY)
    vmem = pl.BlockSpec(memory_space=pltpu.VMEM)
    smem = pl.BlockSpec(memory_space=pltpu.SMEM)
    v = pltpu.VMEM
    scratch = [
        v((8, ROWS, KC), BF16),
        v((8, ROWS, GKC), BF16),
        v((3, 5120, 384), BF16),
        v((3, 4, 4, 2, 64, HD), BF16),
        v((4, 4, 2, 160, 384), BF16),
        v((4, 4, 2, 64, HD), BF16),
        v((2, 2, 160, 64), BF16),
        v((2, 2, 64, 64), BF16),
        v((ROWS, KC), BF16),
        v((ROWS, GKC), BF16),
        v((3, ROWS, 384), F32),
        v((3, ROWS, HD), F32),
        v((3, 4, ROWS, HD), BF16),
        v((4, ROWS, HD), BF16),
        v((2, 4, 2, 4, ROWS, HD), BF16),
        v((3, 1, QT), F32),
        v((3, 1, QT), F32),
        v((3, HD, QT), F32),
        v((4 * ROWS, HD), BF16),
        v((4, 2, 4, ROWS, HD), BF16),
        v((ROWS, TOKENS), BF16),
        v((ROWS, KC), F32),
        v((ROWS, GKC), F32),
        v((8, 8, ROWS), F32),
        v((8, 8, ROWS), F32),
        v((8, 8, ROWS), F32),
        v((8, 8, ROWS), F32),
        v((8, 8, ROWS), F32),
        v((8, 8, ROWS), F32),
        v((4, 4, 2, 8, ROWS), F32),
        v((8, 8, ROWS), F32),
        pltpu.SemaphoreType.DMA((160,)),
        pltpu.SemaphoreType.DMA((160,)),
        pltpu.SemaphoreType.DMA((8,)),
    ]
    guided = pl.pallas_call(
        body,
        out_shape=jax.ShapeDtypeStruct((64, ROWS), F32),
        in_specs=[anyw] * 4 + [vmem] + [anyw] * 5 + [vmem, anyw, vmem, smem],
        out_specs=vmem,
        scratch_shapes=scratch,
        compiler_params=pltpu.CompilerParams(
            collective_id=0, has_side_effects=True, vmem_limit_bytes=56 * 1024 * 1024
        ),
        cost_estimate=pl.CostEstimate(
            flops=6_000_000_000, bytes_accessed=20_000_000, transcendentals=5_000_000
        ),
    )(
        stream, normed, jnp.transpose(qkv_weight, (1, 0, 2)), out_weight.T,
        final_gain.reshape(40, 128), final_weight, guide_stream, guide_normed,
        jnp.transpose(guide_qkv, (1, 0, 2)), guide_out.T, guide_gain.reshape(16, 128), guide_final,
        layout.reshape(48, 128), flags,
    )
    return guided.T


def solution(mesh):
    placed = (
        P("seq", "head"),
        P("seq", "head"),
        P(None, None, "head"),
        P("head", "seq"),
        P(),
        P("seq", None),
        P("seq", "head"),
        P("seq", "head"),
        P("seq", None, "head"),
        P("head", "seq"),
        P(),
        P("seq", None),
        P(),
        P(),
    )
    return jax.shard_map(
        per_device, mesh=mesh, in_specs=placed, out_specs=P("seq", None), check_vma=False
    )
```

```python
import math

import jax
import jax.numpy as jnp
from jax import lax
from jax.experimental import pallas as pl
from jax.experimental.pallas import tpu as pltpu
from jax.sharding import PartitionSpec as P

HD = 128
FRAME_TOK = 512
EPS = 1e-05
TEMPER = 2.5
SCALE2 = TEMPER / math.sqrt(HD) * math.log2(math.e)
F32, BF16 = jnp.float32, jnp.bfloat16
MESH = pl.DeviceIdType.MESH

ROWS = 192
HALF = 96
KC, GKC = 640, 256
TOKENS = 6144
NT = (((1,), (1,)), ((), ()))
TN = (((0,), (0,)), ((), ()))


def body(
    stream, normed, qkv_t, out_t, gain, fin_t, gstream, gnormed, gqkv_t, gout_t, ggain, gfin,
    layout, flags, out,
    xn, gn, qw, gq, wt, gwt, fw, gfw, sb, gsb, acc, gacc, packed, qb, kv, top, tot, ot, ob, at,
    hot, hid, ghid, fin, pg, pm, rg, rm, gp, outb,
    send_sem, recv_sem, local_sem,
):
    s, g = lax.axis_index("seq"), lax.axis_index("head")
    y, zl, c = s // 8, (s // 2) % 4, s % 2
    x, zh = g // 2, g % 2

    def seq_of(yy, zz, cc):
        return yy * 8 + zz * 2 + cc

    def head_of(xx, hh):
        return xx * 2 + hh

    xp, xm, x2 = (x + 1) % 4, (x + 3) % 4, (x + 2) % 4
    yp, ym, y2 = (y + 1) % 4, (y + 3) % 4, (y + 2) % 4
    oc, oh = 1 - c, 1 - zh
    started = []
    count = [0]

    def role():
        count[0] += 1
        return count[0] - 1

    def copy(r, src, dst, ss, gg):
        return pltpu.make_async_remote_copy(
            src_ref=src, dst_ref=dst, send_sem=send_sem.at[r], recv_sem=recv_sem.at[r],
            device_id=(ss, gg), device_id_type=MESH,
        )

    def send(r, src, dst, ss, gg):
        one = copy(r, src, dst, ss, gg)
        one.start()
        started.append(one)

    def wait(r, dst):
        copy(r, dst, dst, seq_of(y, zl, oc), g).wait_recv()

    part_s, part_g = g * 4 + s % 4, s // 4
    same = jnp.logical_and(x == y, zh == zl // 2)
    barrier = pltpu.get_barrier_semaphore()
    peers = [(seq_of(y, (zl + d) % 4, c), g) for d in (1, 2, 3)]
    peers += [(seq_of(y, (zl + d) % 4, c), head_of(x, oh)) for d in (0, 1, 2, 3)]
    peers += [(s, head_of((x + d) % 4, h)) for d in (1, 2, 3) for h in (zh, oh)]
    peers += [(seq_of((y + d) % 4, zl, c), g) for d in (1, 2, 3)]
    peers += [(seq_of(y, (zl + d) % 4, oc), g) for d in (0, 1, 2, 3)]
    for ss, gg in peers:
        pl.semaphore_signal(barrier, inc=1, device_id=(ss, gg), device_id_type=MESH)

    @pl.when(jnp.logical_not(same))
    def _():
        pl.semaphore_signal(barrier, inc=1, device_id=(part_s, part_g), device_id_type=MESH)

    local = [
        (normed, xn.at[g]), (gnormed, gn.at[g]), (gqkv_t, gq.at[:, y, zl, c]),
        (qkv_t, qw), (stream, sb), (gstream, gsb),
    ]
    local = [pltpu.make_async_copy(a, b, local_sem.at[i]) for i, (a, b) in enumerate(local)]
    for one in local:
        one.start()

    token = s * ROWS + lax.broadcasted_iota(jnp.int32, (ROWS, 128), 0)
    for r in range(TOKENS // 128):
        row = layout[pl.ds(r, 1), :]
        hot[:, r * 128 : (r + 1) * 128] = jnp.where(token == row, 1.0, 0.0).astype(BF16)
    fin[...] = fin_t[...].astype(F32).T.astype(BF16)
    for buf in (pg, pm):
        buf[...] = jnp.zeros_like(buf)

    pl.semaphore_wait(barrier, len(peers) + 1 - same.astype(jnp.int32))

    r_gqz = [role() for _ in range(3)]
    for d in (1, 2, 3):
        send(r_gqz[d - 1], gqkv_t, gq.at[:, y, zl, c], seq_of(y, (zl + d) % 4, c), g)
    low, high = pl.ds(0, HALF), pl.ds(HALF, HALF)
    whole = pl.ds(0, ROWS)
    sets = [
        (gn, gnormed, whole, low, high), (xn, normed, low, low, None), (xn, normed, high, None, high),
    ]
    r_cross, r_p, r_m, r_rp, r_rm = (
        [[role(), role()] for _ in sets] for _ in range(5)
    )
    for i, (buf, src, rows, _, _) in enumerate(sets):
        send(r_cross[i][0], src.at[rows], buf.at[g, rows], s, head_of(x, oh))
    for i, (buf, src, rows, _, _) in enumerate(sets):
        send(r_p[i][0], src.at[rows], buf.at[g, rows], s, head_of(xp, zh))
        send(r_m[i][0], src.at[rows], buf.at[g, rows], s, head_of(xm, zh))

    moved = [
        (out_t, wt.at[x, zh * 2 + zl % 2, c], wt.at[y, zl, c]),
        (gout_t, gwt.at[x, zh * 2 + zl % 2, c], gwt.at[y, zl, c]),
        (fin, fw.at[zl % 2, c], fw.at[zl % 2, c]),
        (gfin, gfw.at[zl % 2, c], gfw.at[zl % 2, c]),
    ]
    r_perm = [role() for _ in moved]

    @pl.when(jnp.logical_not(same))
    def _():
        for r, (src, there, _) in zip(r_perm, moved):
            copy(r, src, there, part_s, part_g).start()

    @pl.when(same)
    def _():
        for r, (src, _, here) in zip(r_perm, moved):
            pltpu.make_async_copy(src, here, recv_sem.at[r]).start()

    def relay(i, h):
        buf, _, rows, up, down = sets[i]
        k = 0 if h is zh else 1
        from_m, from_p = head_of(xm, h), head_of(xp, h)
        for first in (True, False) if up is not None else (False, True):
            if first:
                wait(r_p[i][k], buf.at[from_m, rows])
                if up is not None:
                    piece = buf.at[from_m, up]
                    send(r_rp[i][k], piece, piece, s, head_of(xp, zh))
            else:
                wait(r_m[i][k], buf.at[from_p, rows])
                if down is not None:
                    piece = buf.at[from_p, down]
                    send(r_rm[i][k], piece, piece, s, head_of(xm, zh))

    def far(i, h):
        buf, _, _, up, down = sets[i]
        k = 0 if h is zh else 1
        if up is not None:
            wait(r_rp[i][k], buf.at[head_of(x2, h), up])
        if down is not None:
            wait(r_rm[i][k], buf.at[head_of(x2, h), down])

    def onward(i):
        buf, _, rows, _, _ = sets[i]
        other = buf.at[head_of(x, oh), rows]
        wait(r_cross[i][0], other)
        send(r_p[i][1], other, other, s, head_of(xp, zh))
        send(r_m[i][1], other, other, s, head_of(xm, zh))

    def project(gg, first=False):
        rows = xn[gg]
        for i in range(3):
            part = jnp.dot(
                rows, qw[i, pl.ds(pl.multiple_of(gg * KC, KC), KC), :], preferred_element_type=F32
            )
            acc[i] = part if first else acc[i] + part

    def gproject(gg, first=False):
        rows = gn[gg]
        for i in range(3):
            block = gq[i, gg // 2, pl.ds((gg % 2) * 2, 2)].reshape(GKC, HD)
            part = jnp.dot(rows, block, preferred_element_type=F32)
            gacc[i] = part if first else gacc[i] + part

    relay(0, zh)
    onward(0)
    relay(1, zh)
    relay(2, zh)
    local[2].wait()
    for d in (1, 2, 3):
        wait(r_gqz[d - 1], gq.at[:, y, (zl + 4 - d) % 4, c])
    r_gqy, r_gqc = [role() for _ in range(3)], role()
    mine = gq.at[:, y, :, c]
    for d in (1, 3, 2):
        send(r_gqy[d - 1], mine, mine, seq_of((y + d) % 4, zl, c), g)
    onward(1)
    for i in (0, 1, 3):
        local[i].wait()
    project(g, True)
    project(head_of(xm, zh))
    onward(2)
    project(head_of(xp, zh))
    relay(0, oh)
    for d in (1, 2, 3):
        wait(r_gqy[d - 1], gq.at[:, (y + 4 - d) % 4, :, c])
    send(r_gqc, gq.at[:, :, :, c], gq.at[:, :, :, c], seq_of(y, zl, oc), g)
    project(head_of(x, oh))
    for i in range(3):
        far(i, zh)
    relay(1, oh)
    project(head_of(x2, zh))
    relay(2, oh)
    project(head_of(xm, oh))
    project(head_of(xp, oh))
    wait(r_gqc, gq.at[:, :, :, oc])
    gproject(g, True)
    for gg in (head_of(xm, zh), head_of(xp, zh), head_of(x2, zh), head_of(x, oh)):
        gproject(gg)
    gproject(head_of(xm, oh))
    gproject(head_of(xp, oh))
    far(0, oh)
    gproject(head_of(x2, oh))
    far(1, oh)
    far(2, oh)
    project(head_of(x2, oh))
    for i in range(3):
        for j in range(3):
            packed[i, j] = acc[i, :, j * HD : (j + 1) * HD].astype(BF16)
        packed[i, 3] = gacc[i].astype(BF16)

    own = [
        pltpu.make_async_copy(packed.at[0, zl], qb.at[zl], local_sem.at[6]),
        pltpu.make_async_copy(packed.at[1:3, zl], kv.at[:, y, c, zl], local_sem.at[7]),
    ]
    for one in own:
        one.start()
    r_q, r_kv = [role() for _ in range(3)], [role() for _ in range(3)]
    for d in (1, 2, 3):
        j = (zl + d) % 4
        there = seq_of(y, j, c)
        send(r_kv[d - 1], packed.at[1:3, j], kv.at[:, y, c, zl], there, g)
    for d in (1, 2, 3):
        j = (zl + d) % 4
        send(r_q[d - 1], packed.at[0, j], qb.at[zl], seq_of(y, j, c), g)
    for r, (_, _, here) in zip(r_perm, moved):
        wait(r, here)
    r_wz, r_gwz = [role() for _ in range(3)], [role() for _ in range(3)]
    for d in (1, 2, 3):
        there = seq_of(y, (zl + d) % 4, c)
        send(r_wz[d - 1], wt.at[y, zl, c], wt.at[y, zl, c], there, g)
        send(r_gwz[d - 1], gwt.at[y, zl, c], gwt.at[y, zl, c], there, g)
    zn = zl + 1 - 2 * (zl % 2)
    r_fz, r_gfz = role(), role()
    send(r_fz, fw.at[zl % 2, c], fw.at[zl % 2, c], seq_of(y, zn, c), g)
    send(r_gfz, gfw.at[zl % 2, c], gfw.at[zl % 2, c], seq_of(y, zn, c), g)
    r_kp, r_km = [role() for _ in range(4)], [role() for _ in range(4)]
    r_kc, r_kr = [role() for _ in range(4)], [role() for _ in range(4)]
    r_kcm, r_kcp, r_kc2 = role(), role(), role()
    for d in range(4):
        k = (zl + 4 - d) % 4
        block = kv.at[:, y, c, k]
        if d == 0:
            own[1].wait()
        else:
            wait(r_kv[d - 1], block)
        send(r_kp[d], block, block, seq_of(yp, zl, c), g)
        send(r_km[d], block, block, seq_of(ym, zl, c), g)
        send(r_kc[d], block, block, seq_of(y, zl, oc), g)
    own[0].wait()
    for d in (1, 2, 3):
        wait(r_q[d - 1], qb.at[(zl + 4 - d) % 4])

    def absorb(yy, cc, first=False):
        keys = kv[0, yy, cc].reshape(4 * ROWS, HD)
        values = kv[1, yy, cc].reshape(4 * ROWS, HD)
        queries = qb[...].reshape(4 * ROWS, HD)
        scores = lax.dot_general(keys, queries, NT, preferred_element_type=F32)
        highest = jnp.max(scores, axis=0, keepdims=True)
        if not first:
            before = top[...]
            highest = jnp.maximum(highest, before)
        expd = jnp.exp2((scores - highest) * SCALE2)
        total = jnp.sum(expd, axis=0, keepdims=True)
        mixed = lax.dot_general(values, expd.astype(BF16), TN, preferred_element_type=F32)
        top[...] = highest
        if first:
            tot[...] = total
            ot[...] = mixed
        else:
            shrink = jnp.exp2((before - highest) * SCALE2)
            tot[...] = tot[...] * shrink + total
            ot[...] = ot[...] * shrink + mixed

    absorb(y, c, True)
    for d in (0, 1):
        k = (zl + 4 - d) % 4
        wait(r_kp[d], kv.at[:, ym, c, k])
        send(r_kr[d], kv.at[:, ym, c, k], kv.at[:, ym, c, k], seq_of(yp, zl, c), g)
    for d in (2, 3):
        k = (zl + 4 - d) % 4
        wait(r_km[d], kv.at[:, yp, c, k])
        send(r_kr[d], kv.at[:, yp, c, k], kv.at[:, yp, c, k], seq_of(ym, zl, c), g)
    for d in (2, 3):
        wait(r_kp[d], kv.at[:, ym, c, (zl + 4 - d) % 4])
    send(r_kcm, kv.at[:, ym, c], kv.at[:, ym, c], seq_of(y, zl, oc), g)
    for d in (0, 1):
        wait(r_km[d], kv.at[:, yp, c, (zl + 4 - d) % 4])
    send(r_kcp, kv.at[:, yp, c], kv.at[:, yp, c], seq_of(y, zl, oc), g)
    for d in (1, 2, 3):
        wait(r_wz[d - 1], wt.at[y, (zl + 4 - d) % 4, c])
        wait(r_gwz[d - 1], gwt.at[y, (zl + 4 - d) % 4, c])
    r_w = [[role() for _ in range(6)] for _ in range(2)]
    for r, buf in zip(r_w, (wt, gwt)):
        block = buf.at[y, :, c]
        send(r[0], block, block, seq_of(yp, zl, c), g)
        send(r[1], block, block, seq_of(ym, zl, c), g)
    for d in range(4):
        wait(r_kc[d], kv.at[:, y, oc, (zl + 4 - d) % 4])
    absorb(y, oc)
    absorb(ym, c)
    absorb(yp, c)
    for d in range(4):
        wait(r_kr[d], kv.at[:, y2, c, (zl + 4 - d) % 4])
    send(r_kc2, kv.at[:, y2, c], kv.at[:, y2, c], seq_of(y, zl, oc), g)
    wait(r_kcm, kv.at[:, ym, oc])
    absorb(ym, oc)
    wait(r_kcp, kv.at[:, yp, oc])
    absorb(yp, oc)
    absorb(y2, c)
    wait(r_fz, fw.at[1 - zl % 2, c])
    wait(r_gfz, gfw.at[1 - zl % 2, c])
    r_fc, r_gfc = role(), role()
    send(r_fc, fw.at[:, c], fw.at[:, c], seq_of(y, zl, oc), g)
    send(r_gfc, gfw.at[:, c], gfw.at[:, c], seq_of(y, zl, oc), g)
    wait(r_kc2, kv.at[:, y2, oc])
    absorb(y2, oc)
    ob[...] = (ot[...] / tot[...]).T.astype(BF16)

    r_o = [[role(), role()] for _ in range(4)]
    for d in (0, 1, 2, 3):
        k = (zl + d) % 4
        block = ob.at[pl.ds(pl.multiple_of(k * ROWS, ROWS), ROWS), :]
        for e, h in enumerate((zh, oh)):
            if d == 0 and e == 0:
                pltpu.make_async_copy(block, at.at[x, zh, zl], recv_sem.at[r_o[0][0]]).start()
            else:
                send(r_o[d][e], block, at.at[x, zh, zl], seq_of(y, k, c), head_of(x, h))
    first_o = r_o[0][0]

    def arrived(j):
        d = (zl + 4 - j) % 4
        for e, h in enumerate((zh, oh)):
            wait(first_o + d * 2 + e, at.at[x, h, j])

    r_gx = [role() for _ in range(4)]
    r_mx = [role() for _ in range(4)]
    arrived(3)
    send(r_gx[0], at.at[x, :, 3], at.at[x, :, 3], s, head_of(xp, zh))
    send(r_gx[1], at.at[x, :, 3], at.at[x, :, 3], s, head_of(xm, zh))
    for j in range(3):
        arrived(j)
    send(r_mx[0], at.at[x, :, 0:3], at.at[x, :, 0:3], s, head_of(xp, zh))
    send(r_mx[1], at.at[x, :, 0:3], at.at[x, :, 0:3], s, head_of(xm, zh))

    for r, buf in zip(r_w, (wt, gwt)):
        a, b = buf.at[ym, 0:2, c], buf.at[yp, 2:4, c]
        wait(r[0], buf.at[ym, :, c])
        send(r[2], a, a, seq_of(yp, zl, c), g)
        wait(r[1], buf.at[yp, :, c])
        send(r[3], b, b, seq_of(ym, zl, c), g)
    wait(r_gx[0], at.at[xm, :, 3])
    send(r_gx[2], at.at[xm, 0, 3], at.at[xm, 0, 3], s, head_of(xp, zh))
    wait(r_gx[1], at.at[xp, :, 3])
    send(r_gx[3], at.at[xp, 1, 3], at.at[xp, 1, 3], s, head_of(xm, zh))
    wait(r_mx[0], at.at[xm, :, 0:3])
    send(r_mx[2], at.at[xm, 0, 0:3], at.at[xm, 0, 0:3], s, head_of(xp, zh))
    wait(r_mx[1], at.at[xp, :, 0:3])
    send(r_mx[3], at.at[xp, 1, 0:3], at.at[xp, 1, 0:3], s, head_of(xm, zh))
    for r, buf in zip(r_w, (wt, gwt)):
        wait(r[2], buf.at[y2, 0:2, c])
        wait(r[3], buf.at[y2, 2:4, c])
        send(r[4], buf.at[:, :, c], buf.at[:, :, c], seq_of(y, zl, oc), g)
    wait(r_fc, fw.at[:, oc])
    wait(r_gfc, gfw.at[:, oc])
    local[4].wait()
    local[5].wait()

    def gout_part(xx):
        total = None
        for h in range(2):
            block = gwt[xx, h * 2 : h * 2 + 2].reshape(GKC, HD)
            part = lax.dot_general(at[xx, h, 3], block, NT, preferred_element_type=F32)
            total = part if total is None else total + part
        return total

    def out_part(xx):
        total = None
        for h in range(2):
            rows = jnp.concatenate([at[xx, h, j] for j in range(3)], axis=1)
            block = wt[xx, h * 2 : h * 2 + 2].reshape(KC, 3 * HD)
            part = lax.dot_general(rows, block, NT, preferred_element_type=F32)
            total = part if total is None else total + part
        return total

    def column_sums(gains, weights, width, keep):
        n = width // 128
        row = jnp.concatenate([gains[pl.ds(g * n + i, 1), :] for i in range(n)], axis=1)
        rest = row - row.astype(BF16).astype(F32)
        at_row = lax.broadcasted_iota(jnp.int32, (16, width), 0)
        both = jnp.where(at_row == 0, row, jnp.where(at_row == 1, rest, 0.0)).astype(BF16)
        sums = jnp.dot(both, weights[...].reshape(width, 64), preferred_element_type=F32)
        sums = jnp.broadcast_to(jnp.sum(sums, axis=0, keepdims=True), (64, 64)).T
        for i in range(8):
            keep[i, 0:8, ROWS:] = sums[i * 8 : (i + 1) * 8]

    def spread(ref, width, gains, weights, keep, buf, roles):
        one = jnp.zeros((ROWS, 128), F32)
        two = jnp.zeros((ROWS, 128), F32)
        for i in range(width // 128):
            cols = ref[:, i * 128 : (i + 1) * 128]
            one = one + cols
            two = two + cols * cols
        center = jnp.sum(one, axis=1, keepdims=True) * (1.0 / width)
        parts = []
        for i in range(width // 128):
            row = gains[pl.ds(g * (width // 128) + i, 1), :]
            parts.append(((ref[:, i * 128 : (i + 1) * 128] - center) * row).astype(BF16))
        part = jnp.dot(
            jnp.concatenate(parts, axis=1), weights[...].reshape(width, 64),
            preferred_element_type=F32,
        ).T
        one = jnp.sum(one.T, axis=0, keepdims=True)
        two = jnp.sum(two.T, axis=0, keepdims=True)
        for i in range(8):
            keep[i, 0:8, 0:ROWS] = part[i * 8 : (i + 1) * 8]
            keep[i, 8:9, 0:ROWS] = one
            keep[i, 9:10, 0:ROWS] = two
        for d in range(1, 8):
            k = (g + d) % 8
            send(roles[d - 1], keep.at[k], buf.at[g], s, k)
        buf[g] = keep[g]

    def combine(width, buf, roles):
        for d in range(1, 8):
            wait(roles[d - 1], buf.at[(g + 8 - d) % 8])
        one, two = buf[0, 8:9, 0:ROWS], buf[0, 9:10, 0:ROWS]
        for i in range(1, 8):
            one, two = one + buf[i, 8:9, 0:ROWS], two + buf[i, 9:10, 0:ROWS]
        center, square = one * (0.125 / width), two * (0.125 / width)
        scale = lax.rsqrt(square - center * center + EPS)
        total = jnp.zeros((8, ROWS), F32)
        for i in range(8):
            shift = buf[i, 8:9, 0:ROWS] * (1.0 / width) - center
            total = total + (buf[i, 0:8, 0:ROWS] + shift * buf[i, 0:8, ROWS : ROWS + 1])
        return total * scale

    r_pg, r_pm, r_out = ([role() for _ in range(7)] for _ in range(3))
    column_sums(ggain, gfw, GKC, pg)
    column_sums(gain, fw, KC, pm)
    wait(r_w[1][4], gwt.at[:, :, oc])
    ghid[...] = gsb[...].astype(F32) + gout_part(x)
    ghid[...] += gout_part(xm)
    ghid[...] += gout_part(xp)
    wait(r_gx[2], at.at[x2, 0, 3])
    wait(r_gx[3], at.at[x2, 1, 3])
    ghid[...] += gout_part(x2)
    spread(ghid, GKC, ggain, gfw, pg, rg, r_pg)
    wait(r_w[0][4], wt.at[:, :, oc])
    hid[...] = sb[...].astype(F32) + out_part(x)
    hid[...] += out_part(xm)
    hid[...] += out_part(xp)
    gp[y, zl, c] = combine(GKC, rg, r_pg)
    near = [(d, e) for d in range(4) for e in range(2) if d or e]
    r_az, r_ay = [role() for _ in near], [role() for _ in range(3)]
    for r, (d, e) in zip(r_az, near):
        block = gp.at[y, zl, c]
        send(r, block, block, seq_of(y, (zl + d) % 4, oc if e else c), g)
    wait(r_mx[2], at.at[x2, 0, 0:3])
    wait(r_mx[3], at.at[x2, 1, 0:3])
    hid[...] += out_part(x2)
    spread(hid, KC, gain, fw, pm, rm, r_pm)
    for r, (d, e) in zip(r_az, near):
        wait(r, gp.at[y, (zl + 4 - d) % 4, oc if e else c])
    for d in (1, 2, 3):
        send(r_ay[d - 1], gp.at[y], gp.at[y], seq_of((y + d) % 4, zl, c), g)
    main_pred = combine(KC, rm, r_pm)
    for d in (1, 2, 3):
        wait(r_ay[d - 1], gp.at[(y + 4 - d) % 4])

    lane = lax.broadcasted_iota(jnp.int32, (8, 128), 1)
    pieces = []
    for yy in range(4):
        for zz in range(4):
            a0, a1 = gp[yy, zz, 0, :, 0:128], gp[yy, zz, 0, :, 128:192]
            b0, b1 = gp[yy, zz, 1, :, 0:64], gp[yy, zz, 1, :, 64:192]
            pieces += [a0, jnp.concatenate([a1, b0], axis=1), b1]
    slots = jnp.concatenate(pieces, axis=1)
    upper = slots.astype(BF16)
    lower = (slots - upper.astype(F32)).astype(BF16)
    both = jnp.concatenate([upper, lower], axis=0)
    picked = lax.dot_general(both, hot[...], NT, preferred_element_type=F32)
    picked = picked[0:8] + picked[8:16]

    first = s * ROWS
    frame = first // FRAME_TOK
    last = (first + ROWS - 1) // FRAME_TOK
    owned = first + lax.broadcasted_iota(jnp.int32, (8, ROWS), 1)
    strength = 1.0 + jnp.where(owned // FRAME_TOK == frame, flags[frame], flags[last]).astype(F32)
    outb[g] = picked + strength * (main_pred - picked)
    for d in range(1, 8):
        send(r_out[d - 1], outb.at[g], outb.at[g], s, (g + d) % 8)
    for d in range(1, 8):
        wait(r_out[d - 1], outb.at[(g + 8 - d) % 8])
    for i in range(8):
        out[i * 8 : (i + 1) * 8, :] = outb[i]

    for one in started:
        one.wait_send()

    @pl.when(jnp.logical_not(same))
    def _():
        for r, (src, there, _) in zip(r_perm, moved):
            copy(r, src, there, part_s, part_g).wait_send()


def per_device(
    stream, normed, qkv_weight, out_weight, final_gain, final_weight, guide_stream, guide_normed,
    guide_qkv, guide_out, guide_gain, guide_final, layout, flags,
):
    anyw = pl.BlockSpec(memory_space=pl.ANY)
    vmem = pl.BlockSpec(memory_space=pltpu.VMEM)
    smem = pl.BlockSpec(memory_space=pltpu.SMEM)
    v = pltpu.VMEM
    scratch = [
        v((8, ROWS, KC), BF16),
        v((8, ROWS, GKC), BF16),
        v((3, 5120, 384), BF16),
        v((3, 4, 4, 2, 64, HD), BF16),
        v((4, 4, 2, 160, 384), BF16),
        v((4, 4, 2, 64, HD), BF16),
        v((2, 2, 160, 64), BF16),
        v((2, 2, 64, 64), BF16),
        v((ROWS, KC), BF16),
        v((ROWS, GKC), BF16),
        v((3, ROWS, 384), F32),
        v((3, ROWS, HD), F32),
        v((3, 4, ROWS, HD), BF16),
        v((4, ROWS, HD), BF16),
        v((2, 4, 2, 4, ROWS, HD), BF16),
        v((1, 4 * ROWS), F32),
        v((1, 4 * ROWS), F32),
        v((HD, 4 * ROWS), F32),
        v((4 * ROWS, HD), BF16),
        v((4, 2, 4, ROWS, HD), BF16),
        v((ROWS, TOKENS), BF16),
        v((ROWS, KC), F32),
        v((ROWS, GKC), F32),
        v((160, 64), BF16),
        v((8, 16, 256), F32),
        v((8, 16, 256), F32),
        v((8, 16, 256), F32),
        v((8, 16, 256), F32),
        v((4, 4, 2, 8, ROWS), F32),
        v((8, 8, ROWS), F32),
        pltpu.SemaphoreType.DMA((192,)),
        pltpu.SemaphoreType.DMA((192,)),
        pltpu.SemaphoreType.DMA((8,)),
    ]
    guided = pl.pallas_call(
        body,
        out_shape=jax.ShapeDtypeStruct((64, ROWS), F32),
        in_specs=[anyw] * 4 + [vmem, vmem] + [anyw] * 4 + [vmem, anyw, vmem, smem],
        out_specs=vmem,
        scratch_shapes=scratch,
        compiler_params=pltpu.CompilerParams(
            collective_id=0, has_side_effects=True, vmem_limit_bytes=56 * 1024 * 1024
        ),
        cost_estimate=pl.CostEstimate(
            flops=6_000_000_000, bytes_accessed=20_000_000, transcendentals=5_000_000
        ),
    )(
        stream, normed, jnp.transpose(qkv_weight, (1, 0, 2)), out_weight.T,
        final_gain.reshape(40, 128), final_weight.T, guide_stream, guide_normed,
        jnp.transpose(guide_qkv, (1, 0, 2)), guide_out.T, guide_gain.reshape(16, 128), guide_final,
        layout.reshape(48, 128), flags,
    )
    return guided.T


def solution(mesh):
    placed = (
        P("seq", "head"),
        P("seq", "head"),
        P(None, None, "head"),
        P("head", "seq"),
        P(),
        P("seq", None),
        P("seq", "head"),
        P("seq", "head"),
        P("seq", None, "head"),
        P("head", "seq"),
        P(),
        P("seq", None),
        P(),
        P(),
    )
    return jax.shard_map(
        per_device, mesh=mesh, in_specs=placed, out_specs=P("seq", None), check_vma=False
    )
```

```python
import math

import jax
import jax.numpy as jnp
from jax import lax
from jax.experimental import pallas as pl
from jax.experimental.pallas import tpu as pltpu
from jax.sharding import PartitionSpec as P

HD = 128
FRAME_TOK = 512
EPS = 1e-05
TEMPER = 2.5
SCALE2 = TEMPER / math.sqrt(HD) * math.log2(math.e)
F32, BF16 = jnp.float32, jnp.bfloat16
MESH = pl.DeviceIdType.MESH

ROWS = 192
HALF = 96
KC, GKC = 640, 256
TOKENS = 6144
NT = (((1,), (1,)), ((), ()))
TN = (((0,), (0,)), ((), ()))


def body(
    stream, normed, qkv_t, out_t, gain, fin_t, gstream, gnormed, gqkv_t, gout_t, ggain, gfin,
    layout, flags, out,
    xn, gn, qw, gq, wt, gwt, fw, gfw, sb, gsb, acc, gacc, packed, qb, kv, top, tot, ot, ob, at,
    hot, hid, ghid, fin, pg, pm, rg, rm, gp, outb,
    send_sem, recv_sem, local_sem,
):
    s, g = lax.axis_index("seq"), lax.axis_index("head")
    y, zl, c = s // 8, (s // 2) % 4, s % 2
    x, zh = g // 2, g % 2

    def seq_of(yy, zz, cc):
        return yy * 8 + zz * 2 + cc

    def head_of(xx, hh):
        return xx * 2 + hh

    xp, xm, x2 = (x + 1) % 4, (x + 3) % 4, (x + 2) % 4
    yp, ym, y2 = (y + 1) % 4, (y + 3) % 4, (y + 2) % 4
    oc, oh = 1 - c, 1 - zh
    started = []
    count = [0]

    def role():
        count[0] += 1
        return count[0] - 1

    def copy(r, src, dst, ss, gg):
        return pltpu.make_async_remote_copy(
            src_ref=src, dst_ref=dst, send_sem=send_sem.at[r], recv_sem=recv_sem.at[r],
            device_id=(ss, gg), device_id_type=MESH,
        )

    def send(r, src, dst, ss, gg):
        one = copy(r, src, dst, ss, gg)
        one.start()
        started.append(one)

    def flush(upto):
        for one in started[:upto]:
            one.wait_send()
        del started[:upto]

    def wait(r, dst):
        copy(r, dst, dst, seq_of(y, zl, oc), g).wait_recv()

    part_s, part_g = g * 4 + s % 4, s // 4
    same = jnp.logical_and(x == y, zh == zl // 2)
    barrier = pltpu.get_barrier_semaphore()
    peers = [(seq_of(y, (zl + d) % 4, c), g) for d in (1, 2, 3)]
    peers += [(seq_of(y, (zl + d) % 4, c), head_of(x, oh)) for d in (0, 1, 2, 3)]
    peers += [(s, head_of((x + d) % 4, h)) for d in (1, 2, 3) for h in (zh, oh)]
    peers += [(seq_of((y + d) % 4, zl, c), g) for d in (1, 2, 3)]
    peers += [(seq_of(y, (zl + d) % 4, oc), g) for d in (0, 1, 2, 3)]
    for ss, gg in peers:
        pl.semaphore_signal(barrier, inc=1, device_id=(ss, gg), device_id_type=MESH)

    @pl.when(jnp.logical_not(same))
    def _():
        pl.semaphore_signal(barrier, inc=1, device_id=(part_s, part_g), device_id_type=MESH)

    local = [
        (normed, xn.at[g]), (gnormed, gn.at[g]), (gqkv_t, gq.at[:, y, zl, c]),
        (qkv_t, qw), (stream, sb), (gstream, gsb),
    ]
    local = [pltpu.make_async_copy(a, b, local_sem.at[i]) for i, (a, b) in enumerate(local)]
    for one in local:
        one.start()

    token = s * ROWS + lax.broadcasted_iota(jnp.int32, (ROWS, 128), 0)
    for r in range(TOKENS // 128):
        row = layout[pl.ds(r, 1), :]
        hot[:, r * 128 : (r + 1) * 128] = jnp.where(token == row, 1.0, 0.0).astype(BF16)
    fin[...] = fin_t[...].astype(F32).T.astype(BF16)
    for buf in (pg, pm):
        buf[...] = jnp.zeros_like(buf)

    pl.semaphore_wait(barrier, len(peers) + 1 - same.astype(jnp.int32))

    r_gqz = [role() for _ in range(3)]
    for d in (1, 2, 3):
        send(r_gqz[d - 1], gqkv_t, gq.at[:, y, zl, c], seq_of(y, (zl + d) % 4, c), g)
    low, high = pl.ds(0, HALF), pl.ds(HALF, HALF)
    whole = pl.ds(0, ROWS)
    sets = [
        (gn, gnormed, whole, low, high), (xn, normed, low, low, None), (xn, normed, high, None, high),
    ]
    r_cross, r_p, r_m, r_rp, r_rm = (
        [[role(), role()] for _ in sets] for _ in range(5)
    )
    for i, (buf, src, rows, _, _) in enumerate(sets):
        send(r_cross[i][0], src.at[rows], buf.at[g, rows], s, head_of(x, oh))
    for i, (buf, src, rows, _, _) in enumerate(sets):
        send(r_p[i][0], src.at[rows], buf.at[g, rows], s, head_of(xp, zh))
        send(r_m[i][0], src.at[rows], buf.at[g, rows], s, head_of(xm, zh))

    moved = [
        (out_t, wt.at[x, zh * 2 + zl % 2, c], wt.at[y, zl, c]),
        (gout_t, gwt.at[x, zh * 2 + zl % 2, c], gwt.at[y, zl, c]),
        (fin, fw.at[zl % 2, c], fw.at[zl % 2, c]),
        (gfin, gfw.at[zl % 2, c], gfw.at[zl % 2, c]),
    ]
    r_perm = [role() for _ in moved]

    @pl.when(jnp.logical_not(same))
    def _():
        for r, (src, there, _) in zip(r_perm, moved):
            copy(r, src, there, part_s, part_g).start()

    @pl.when(same)
    def _():
        for r, (src, _, here) in zip(r_perm, moved):
            pltpu.make_async_copy(src, here, recv_sem.at[r]).start()

    def relay(i, h):
        buf, _, rows, up, down = sets[i]
        k = 0 if h is zh else 1
        from_m, from_p = head_of(xm, h), head_of(xp, h)
        for first in (True, False) if up is not None else (False, True):
            if first:
                wait(r_p[i][k], buf.at[from_m, rows])
                if up is not None:
                    piece = buf.at[from_m, up]
                    send(r_rp[i][k], piece, piece, s, head_of(xp, zh))
            else:
                wait(r_m[i][k], buf.at[from_p, rows])
                if down is not None:
                    piece = buf.at[from_p, down]
                    send(r_rm[i][k], piece, piece, s, head_of(xm, zh))

    def far(i, h):
        buf, _, _, up, down = sets[i]
        k = 0 if h is zh else 1
        if up is not None:
            wait(r_rp[i][k], buf.at[head_of(x2, h), up])
        if down is not None:
            wait(r_rm[i][k], buf.at[head_of(x2, h), down])

    def onward(i):
        buf, _, rows, _, _ = sets[i]
        other = buf.at[head_of(x, oh), rows]
        wait(r_cross[i][0], other)
        send(r_p[i][1], other, other, s, head_of(xp, zh))
        send(r_m[i][1], other, other, s, head_of(xm, zh))

    def project(gg, first=False):
        rows = xn[gg]
        for i in range(3):
            part = jnp.dot(
                rows, qw[i, pl.ds(pl.multiple_of(gg * KC, KC), KC), :], preferred_element_type=F32
            )
            acc[i] = part if first else acc[i] + part

    def gproject(gg, first=False):
        rows = gn[gg]
        for i in range(3):
            block = gq[i, gg // 2, pl.ds((gg % 2) * 2, 2)].reshape(GKC, HD)
            part = jnp.dot(rows, block, preferred_element_type=F32)
            gacc[i] = part if first else gacc[i] + part

    local[2].wait()
    for d in (1, 2, 3):
        wait(r_gqz[d - 1], gq.at[:, y, (zl + 4 - d) % 4, c])
    r_gqy, r_gqc = [role() for _ in range(3)], role()
    mine = gq.at[:, y, :, c]
    for d in (1, 3, 2):
        send(r_gqy[d - 1], mine, mine, seq_of((y + d) % 4, zl, c), g)
    relay(0, zh)
    onward(0)
    relay(1, zh)
    relay(2, zh)
    onward(1)
    for i in (0, 1, 3):
        local[i].wait()
    project(g, True)
    project(head_of(xm, zh))
    onward(2)
    for d in (1, 2, 3):
        wait(r_gqy[d - 1], gq.at[:, (y + 4 - d) % 4, :, c])
    send(r_gqc, gq.at[:, :, :, c], gq.at[:, :, :, c], seq_of(y, zl, oc), g)
    for r, (_, _, here) in zip(r_perm, moved):
        wait(r, here)
    r_wz, r_gwz = [role() for _ in range(3)], [role() for _ in range(3)]
    for d in (1, 2, 3):
        there = seq_of(y, (zl + d) % 4, c)
        send(r_wz[d - 1], wt.at[y, zl, c], wt.at[y, zl, c], there, g)
        send(r_gwz[d - 1], gwt.at[y, zl, c], gwt.at[y, zl, c], there, g)
    zn = zl + 1 - 2 * (zl % 2)
    r_fz, r_gfz = role(), role()
    send(r_fz, fw.at[zl % 2, c], fw.at[zl % 2, c], seq_of(y, zn, c), g)
    send(r_gfz, gfw.at[zl % 2, c], gfw.at[zl % 2, c], seq_of(y, zn, c), g)
    project(head_of(xp, zh))
    relay(0, oh)
    project(head_of(x, oh))
    for i in range(3):
        far(i, zh)
    relay(1, oh)
    project(head_of(x2, zh))
    relay(2, oh)
    project(head_of(xm, oh))
    project(head_of(xp, oh))
    wait(r_gqc, gq.at[:, :, :, oc])
    gproject(g, True)
    for gg in (head_of(xm, zh), head_of(xp, zh), head_of(x2, zh), head_of(x, oh)):
        gproject(gg)
    gproject(head_of(xm, oh))
    gproject(head_of(xp, oh))
    far(0, oh)
    gproject(head_of(x2, oh))
    far(1, oh)
    far(2, oh)
    project(head_of(x2, oh))
    for i in range(3):
        for j in range(3):
            packed[i, j] = acc[i, :, j * HD : (j + 1) * HD].astype(BF16)
        packed[i, 3] = gacc[i].astype(BF16)

    sent_a = len(started)

    own = [
        pltpu.make_async_copy(packed.at[0, zl], qb.at[zl], local_sem.at[6]),
        pltpu.make_async_copy(packed.at[1:3, zl], kv.at[:, y, c, zl], local_sem.at[7]),
    ]
    for one in own:
        one.start()
    r_q, r_kv = [role() for _ in range(3)], [role() for _ in range(3)]
    for d in (1, 2, 3):
        j = (zl + d) % 4
        there = seq_of(y, j, c)
        send(r_kv[d - 1], packed.at[1:3, j], kv.at[:, y, c, zl], there, g)
    for d in (1, 2, 3):
        j = (zl + d) % 4
        send(r_q[d - 1], packed.at[0, j], qb.at[zl], seq_of(y, j, c), g)
    r_kp, r_km = [role() for _ in range(4)], [role() for _ in range(4)]
    r_kc, r_kr = [role() for _ in range(4)], [role() for _ in range(4)]
    r_kcm, r_kcp, r_kc2 = role(), role(), role()
    for d in range(4):
        k = (zl + 4 - d) % 4
        block = kv.at[:, y, c, k]
        if d == 0:
            own[1].wait()
        else:
            wait(r_kv[d - 1], block)
        send(r_kp[d], block, block, seq_of(yp, zl, c), g)
        send(r_km[d], block, block, seq_of(ym, zl, c), g)
        send(r_kc[d], block, block, seq_of(y, zl, oc), g)
    own[0].wait()
    for d in (1, 2, 3):
        wait(r_q[d - 1], qb.at[(zl + 4 - d) % 4])

    def absorb(yy, cc, first=False):
        keys = kv[0, yy, cc].reshape(4 * ROWS, HD)
        values = kv[1, yy, cc].reshape(4 * ROWS, HD)
        queries = qb[...].reshape(4 * ROWS, HD)
        scores = lax.dot_general(keys, queries, NT, preferred_element_type=F32)
        highest = jnp.max(scores, axis=0, keepdims=True)
        if not first:
            before = top[...]
            highest = jnp.maximum(highest, before)
        expd = jnp.exp2((scores - highest) * SCALE2)
        total = jnp.sum(expd, axis=0, keepdims=True)
        mixed = lax.dot_general(values, expd.astype(BF16), TN, preferred_element_type=F32)
        top[...] = highest
        if first:
            tot[...] = total
            ot[...] = mixed
        else:
            shrink = jnp.exp2((before - highest) * SCALE2)
            tot[...] = tot[...] * shrink + total
            ot[...] = ot[...] * shrink + mixed

    absorb(y, c, True)
    for d in (0, 1):
        k = (zl + 4 - d) % 4
        wait(r_kp[d], kv.at[:, ym, c, k])
        send(r_kr[d], kv.at[:, ym, c, k], kv.at[:, ym, c, k], seq_of(yp, zl, c), g)
    for d in (2, 3):
        k = (zl + 4 - d) % 4
        wait(r_km[d], kv.at[:, yp, c, k])
        send(r_kr[d], kv.at[:, yp, c, k], kv.at[:, yp, c, k], seq_of(ym, zl, c), g)
    for d in (2, 3):
        wait(r_kp[d], kv.at[:, ym, c, (zl + 4 - d) % 4])
    send(r_kcm, kv.at[:, ym, c], kv.at[:, ym, c], seq_of(y, zl, oc), g)
    for d in (0, 1):
        wait(r_km[d], kv.at[:, yp, c, (zl + 4 - d) % 4])
    send(r_kcp, kv.at[:, yp, c], kv.at[:, yp, c], seq_of(y, zl, oc), g)
    for d in (1, 2, 3):
        wait(r_wz[d - 1], wt.at[y, (zl + 4 - d) % 4, c])
        wait(r_gwz[d - 1], gwt.at[y, (zl + 4 - d) % 4, c])
    r_w = [[role() for _ in range(6)] for _ in range(2)]
    for r, buf in zip(r_w, (wt, gwt)):
        block = buf.at[y, :, c]
        send(r[0], block, block, seq_of(yp, zl, c), g)
        send(r[1], block, block, seq_of(ym, zl, c), g)
    for d in range(4):
        wait(r_kc[d], kv.at[:, y, oc, (zl + 4 - d) % 4])
    absorb(y, oc)
    absorb(ym, c)
    absorb(yp, c)
    for d in range(4):
        wait(r_kr[d], kv.at[:, y2, c, (zl + 4 - d) % 4])
    send(r_kc2, kv.at[:, y2, c], kv.at[:, y2, c], seq_of(y, zl, oc), g)
    wait(r_kcm, kv.at[:, ym, oc])
    absorb(ym, oc)
    wait(r_kcp, kv.at[:, yp, oc])
    absorb(yp, oc)
    absorb(y2, c)
    wait(r_fz, fw.at[1 - zl % 2, c])
    wait(r_gfz, gfw.at[1 - zl % 2, c])
    r_fc, r_gfc = role(), role()
    send(r_fc, fw.at[:, c], fw.at[:, c], seq_of(y, zl, oc), g)
    send(r_gfc, gfw.at[:, c], gfw.at[:, c], seq_of(y, zl, oc), g)
    flush(sent_a)
    wait(r_kc2, kv.at[:, y2, oc])
    absorb(y2, oc)
    ob[...] = (ot[...] / tot[...]).T.astype(BF16)

    r_o = [[role(), role()] for _ in range(4)]
    for d in (0, 1, 2, 3):
        k = (zl + d) % 4
        block = ob.at[pl.ds(pl.multiple_of(k * ROWS, ROWS), ROWS), :]
        for e, h in enumerate((zh, oh)):
            if d == 0 and e == 0:
                pltpu.make_async_copy(block, at.at[x, zh, zl], recv_sem.at[r_o[0][0]]).start()
            else:
                send(r_o[d][e], block, at.at[x, zh, zl], seq_of(y, k, c), head_of(x, h))
    first_o = r_o[0][0]

    def arrived(j):
        d = (zl + 4 - j) % 4
        for e, h in enumerate((zh, oh)):
            wait(first_o + d * 2 + e, at.at[x, h, j])

    r_gx = [role() for _ in range(4)]
    r_mx = [role() for _ in range(4)]
    arrived(3)
    send(r_gx[0], at.at[x, :, 3], at.at[x, :, 3], s, head_of(xp, zh))
    send(r_gx[1], at.at[x, :, 3], at.at[x, :, 3], s, head_of(xm, zh))
    for j in range(3):
        arrived(j)
    send(r_mx[0], at.at[x, :, 0:3], at.at[x, :, 0:3], s, head_of(xp, zh))
    send(r_mx[1], at.at[x, :, 0:3], at.at[x, :, 0:3], s, head_of(xm, zh))

    for r, buf in zip(r_w, (wt, gwt)):
        a, b = buf.at[ym, 0:2, c], buf.at[yp, 2:4, c]
        wait(r[0], buf.at[ym, :, c])
        send(r[2], a, a, seq_of(yp, zl, c), g)
        wait(r[1], buf.at[yp, :, c])
        send(r[3], b, b, seq_of(ym, zl, c), g)
    wait(r_gx[0], at.at[xm, :, 3])
    send(r_gx[2], at.at[xm, 0, 3], at.at[xm, 0, 3], s, head_of(xp, zh))
    wait(r_gx[1], at.at[xp, :, 3])
    send(r_gx[3], at.at[xp, 1, 3], at.at[xp, 1, 3], s, head_of(xm, zh))
    wait(r_mx[0], at.at[xm, :, 0:3])
    send(r_mx[2], at.at[xm, 0, 0:3], at.at[xm, 0, 0:3], s, head_of(xp, zh))
    wait(r_mx[1], at.at[xp, :, 0:3])
    send(r_mx[3], at.at[xp, 1, 0:3], at.at[xp, 1, 0:3], s, head_of(xm, zh))
    for r, buf in zip(r_w, (wt, gwt)):
        wait(r[2], buf.at[y2, 0:2, c])
        wait(r[3], buf.at[y2, 2:4, c])
        send(r[4], buf.at[:, :, c], buf.at[:, :, c], seq_of(y, zl, oc), g)
    wait(r_fc, fw.at[:, oc])
    wait(r_gfc, gfw.at[:, oc])
    local[4].wait()
    local[5].wait()

    def gout_part(xx):
        total = None
        for h in range(2):
            block = gwt[xx, h * 2 : h * 2 + 2].reshape(GKC, HD)
            part = lax.dot_general(at[xx, h, 3], block, NT, preferred_element_type=F32)
            total = part if total is None else total + part
        return total

    def out_part(xx):
        total = None
        for h in range(2):
            rows = jnp.concatenate([at[xx, h, j] for j in range(3)], axis=1)
            block = wt[xx, h * 2 : h * 2 + 2].reshape(KC, 3 * HD)
            part = lax.dot_general(rows, block, NT, preferred_element_type=F32)
            total = part if total is None else total + part
        return total

    def column_sums(gains, weights, width, keep):
        n = width // 128
        row = jnp.concatenate([gains[pl.ds(g * n + i, 1), :] for i in range(n)], axis=1)
        rest = row - row.astype(BF16).astype(F32)
        at_row = lax.broadcasted_iota(jnp.int32, (16, width), 0)
        both = jnp.where(at_row == 0, row, jnp.where(at_row == 1, rest, 0.0)).astype(BF16)
        sums = jnp.dot(both, weights[...].reshape(width, 64), preferred_element_type=F32)
        sums = jnp.broadcast_to(jnp.sum(sums, axis=0, keepdims=True), (64, 64)).T
        for i in range(8):
            keep[i, 0:8, ROWS:] = sums[i * 8 : (i + 1) * 8]

    def spread(ref, width, gains, weights, keep, buf, roles):
        one = jnp.zeros((ROWS, 128), F32)
        two = jnp.zeros((ROWS, 128), F32)
        for i in range(width // 128):
            cols = ref[:, i * 128 : (i + 1) * 128]
            one = one + cols
            two = two + cols * cols
        center = jnp.sum(one, axis=1, keepdims=True) * (1.0 / width)
        parts = []
        for i in range(width // 128):
            row = gains[pl.ds(g * (width // 128) + i, 1), :]
            parts.append(((ref[:, i * 128 : (i + 1) * 128] - center) * row).astype(BF16))
        part = jnp.dot(
            jnp.concatenate(parts, axis=1), weights[...].reshape(width, 64),
            preferred_element_type=F32,
        ).T
        one = jnp.sum(one.T, axis=0, keepdims=True)
        two = jnp.sum(two.T, axis=0, keepdims=True)
        for i in range(8):
            keep[i, 0:8, 0:ROWS] = part[i * 8 : (i + 1) * 8]
            keep[i, 8:9, 0:ROWS] = one
            keep[i, 9:10, 0:ROWS] = two
        for d in range(1, 8):
            k = (g + d) % 8
            send(roles[d - 1], keep.at[k], buf.at[g], s, k)
        buf[g] = keep[g]

    def combine(width, buf, roles):
        for d in range(1, 8):
            wait(roles[d - 1], buf.at[(g + 8 - d) % 8])
        one, two = buf[0, 8:9, 0:ROWS], buf[0, 9:10, 0:ROWS]
        for i in range(1, 8):
            one, two = one + buf[i, 8:9, 0:ROWS], two + buf[i, 9:10, 0:ROWS]
        center, square = one * (0.125 / width), two * (0.125 / width)
        scale = lax.rsqrt(square - center * center + EPS)
        total = jnp.zeros((8, ROWS), F32)
        for i in range(8):
            shift = buf[i, 8:9, 0:ROWS] * (1.0 / width) - center
            total = total + (buf[i, 0:8, 0:ROWS] + shift * buf[i, 0:8, ROWS : ROWS + 1])
        return total * scale

    r_pg, r_pm, r_out = ([role() for _ in range(7)] for _ in range(3))
    sent_d = len(started)
    column_sums(ggain, gfw, GKC, pg)
    column_sums(gain, fw, KC, pm)
    wait(r_w[1][4], gwt.at[:, :, oc])
    ghid[...] = gsb[...].astype(F32) + gout_part(x)
    ghid[...] += gout_part(xm)
    ghid[...] += gout_part(xp)
    wait(r_gx[2], at.at[x2, 0, 3])
    wait(r_gx[3], at.at[x2, 1, 3])
    ghid[...] += gout_part(x2)
    spread(ghid, GKC, ggain, gfw, pg, rg, r_pg)
    wait(r_w[0][4], wt.at[:, :, oc])
    hid[...] = sb[...].astype(F32) + out_part(x)
    hid[...] += out_part(xm)
    hid[...] += out_part(xp)
    gp[y, zl, c] = combine(GKC, rg, r_pg)
    near = [(d, e) for d in range(4) for e in range(2) if d or e]
    r_az, r_ay = [role() for _ in near], [role() for _ in range(3)]
    for r, (d, e) in zip(r_az, near):
        block = gp.at[y, zl, c]
        send(r, block, block, seq_of(y, (zl + d) % 4, oc if e else c), g)
    wait(r_mx[2], at.at[x2, 0, 0:3])
    wait(r_mx[3], at.at[x2, 1, 0:3])
    hid[...] += out_part(x2)
    spread(hid, KC, gain, fw, pm, rm, r_pm)
    flush(sent_d)

    @pl.when(jnp.logical_not(same))
    def _():
        for r, (src, there, _) in zip(r_perm, moved):
            copy(r, src, there, part_s, part_g).wait_send()

    for r, (d, e) in zip(r_az, near):
        wait(r, gp.at[y, (zl + 4 - d) % 4, oc if e else c])
    for d in (1, 2, 3):
        send(r_ay[d - 1], gp.at[y], gp.at[y], seq_of((y + d) % 4, zl, c), g)
    main_pred = combine(KC, rm, r_pm)
    for d in (1, 2, 3):
        wait(r_ay[d - 1], gp.at[(y + 4 - d) % 4])

    lane = lax.broadcasted_iota(jnp.int32, (8, 128), 1)
    pieces = []
    for yy in range(4):
        for zz in range(4):
            a0, a1 = gp[yy, zz, 0, :, 0:128], gp[yy, zz, 0, :, 128:192]
            b0, b1 = gp[yy, zz, 1, :, 0:64], gp[yy, zz, 1, :, 64:192]
            pieces += [a0, jnp.concatenate([a1, b0], axis=1), b1]
    slots = jnp.concatenate(pieces, axis=1)
    upper = slots.astype(BF16)
    lower = (slots - upper.astype(F32)).astype(BF16)
    both = jnp.concatenate([upper, lower], axis=0)
    picked = lax.dot_general(both, hot[...], NT, preferred_element_type=F32)
    picked = picked[0:8] + picked[8:16]

    first = s * ROWS
    frame = first // FRAME_TOK
    last = (first + ROWS - 1) // FRAME_TOK
    owned = first + lax.broadcasted_iota(jnp.int32, (8, ROWS), 1)
    strength = 1.0 + jnp.where(owned // FRAME_TOK == frame, flags[frame], flags[last]).astype(F32)
    outb[g] = picked + strength * (main_pred - picked)
    for d in range(1, 8):
        send(r_out[d - 1], outb.at[g], outb.at[g], s, (g + d) % 8)
    flush(len(started) - 7)
    for d in range(1, 8):
        wait(r_out[d - 1], outb.at[(g + 8 - d) % 8])
    for i in range(8):
        out[i * 8 : (i + 1) * 8, :] = outb[i]

    flush(len(started))


def per_device(
    stream, normed, qkv_weight, out_weight, final_gain, final_weight, guide_stream, guide_normed,
    guide_qkv, guide_out, guide_gain, guide_final, layout, flags,
):
    anyw = pl.BlockSpec(memory_space=pl.ANY)
    vmem = pl.BlockSpec(memory_space=pltpu.VMEM)
    smem = pl.BlockSpec(memory_space=pltpu.SMEM)
    v = pltpu.VMEM
    scratch = [
        v((8, ROWS, KC), BF16),
        v((8, ROWS, GKC), BF16),
        v((3, 5120, 384), BF16),
        v((3, 4, 4, 2, 64, HD), BF16),
        v((4, 4, 2, 160, 384), BF16),
        v((4, 4, 2, 64, HD), BF16),
        v((2, 2, 160, 64), BF16),
        v((2, 2, 64, 64), BF16),
        v((ROWS, KC), BF16),
        v((ROWS, GKC), BF16),
        v((3, ROWS, 384), F32),
        v((3, ROWS, HD), F32),
        v((3, 4, ROWS, HD), BF16),
        v((4, ROWS, HD), BF16),
        v((2, 4, 2, 4, ROWS, HD), BF16),
        v((1, 4 * ROWS), F32),
        v((1, 4 * ROWS), F32),
        v((HD, 4 * ROWS), F32),
        v((4 * ROWS, HD), BF16),
        v((4, 2, 4, ROWS, HD), BF16),
        v((ROWS, TOKENS), BF16),
        v((ROWS, KC), F32),
        v((ROWS, GKC), F32),
        v((160, 64), BF16),
        v((8, 16, 256), F32),
        v((8, 16, 256), F32),
        v((8, 16, 256), F32),
        v((8, 16, 256), F32),
        v((4, 4, 2, 8, ROWS), F32),
        v((8, 8, ROWS), F32),
        pltpu.SemaphoreType.DMA((192,)),
        pltpu.SemaphoreType.DMA((192,)),
        pltpu.SemaphoreType.DMA((8,)),
    ]
    guided = pl.pallas_call(
        body,
        out_shape=jax.ShapeDtypeStruct((64, ROWS), F32),
        in_specs=[anyw] * 4 + [vmem, vmem] + [anyw] * 4 + [vmem, anyw, vmem, smem],
        out_specs=vmem,
        scratch_shapes=scratch,
        compiler_params=pltpu.CompilerParams(
            collective_id=0, has_side_effects=True, vmem_limit_bytes=56 * 1024 * 1024
        ),
        cost_estimate=pl.CostEstimate(
            flops=6_000_000_000, bytes_accessed=20_000_000, transcendentals=5_000_000
        ),
    )(
        stream, normed, jnp.transpose(qkv_weight, (1, 0, 2)), out_weight.T,
        final_gain.reshape(40, 128), final_weight.T, guide_stream, guide_normed,
        jnp.transpose(guide_qkv, (1, 0, 2)), guide_out.T, guide_gain.reshape(16, 128), guide_final,
        layout.reshape(48, 128), flags,
    )
    return guided.T


def solution(mesh):
    placed = (
        P("seq", "head"),
        P("seq", "head"),
        P(None, None, "head"),
        P("head", "seq"),
        P(),
        P("seq", None),
        P("seq", "head"),
        P("seq", "head"),
        P("seq", None, "head"),
        P("head", "seq"),
        P(),
        P("seq", None),
        P(),
        P(),
    )
    return jax.shard_map(
        per_device, mesh=mesh, in_specs=placed, out_specs=P("seq", None), check_vma=False
    )
```

```python
import math

import jax
import jax.numpy as jnp
from jax import lax
from jax.experimental import pallas as pl
from jax.experimental.pallas import tpu as pltpu
from jax.sharding import PartitionSpec as P

HD = 128
FRAME_TOK = 512
EPS = 1e-05
TEMPER = 2.5
SCALE2 = TEMPER / math.sqrt(HD) * math.log2(math.e)
F32, BF16 = jnp.float32, jnp.bfloat16
MESH = pl.DeviceIdType.MESH

ROWS = 192
HALF = 96
KC, GKC = 640, 256
TOKENS = 6144
NT = (((1,), (1,)), ((), ()))
TN = (((0,), (0,)), ((), ()))


def body(
    stream, normed, qkv_t, out_t, gain, fin_t, gstream, gnormed, gqkv_t, gout_t, ggain, gfin,
    layout, flags, out,
    xn, gn, qw, gq, wt, gwt, fw, gfw, sb, gsb, acc, gacc, packed, qb, kv, top, tot, ot, ob, at,
    hot, hid, ghid, fin, pg, pm, rg, rm, gp, outb,
    send_sem, recv_sem, local_sem,
):
    s, g = lax.axis_index("seq"), lax.axis_index("head")
    y, zl, c = s // 8, (s // 2) % 4, s % 2
    x, zh = g // 2, g % 2

    def seq_of(yy, zz, cc):
        return yy * 8 + zz * 2 + cc

    def head_of(xx, hh):
        return xx * 2 + hh

    xp, xm, x2 = (x + 1) % 4, (x + 3) % 4, (x + 2) % 4
    yp, ym, y2 = (y + 1) % 4, (y + 3) % 4, (y + 2) % 4
    oc, oh = 1 - c, 1 - zh
    started = []
    count = [0]

    def role():
        count[0] += 1
        return count[0] - 1

    def copy(r, src, dst, ss, gg):
        return pltpu.make_async_remote_copy(
            src_ref=src, dst_ref=dst, send_sem=send_sem.at[r], recv_sem=recv_sem.at[r],
            device_id=(ss, gg), device_id_type=MESH,
        )

    def send(r, src, dst, ss, gg):
        one = copy(r, src, dst, ss, gg)
        one.start()
        started.append(one)

    maybe = []

    def line(block, own):
        up, down = [role() for _ in range(3)], [role() for _ in range(3)]

        def give(when, r, src, dst, zz):
            @pl.when(when)
            def _():
                copy(r, src, dst, seq_of(y, zz, c), g).start()

            maybe.append((when, r, dst, zz))

        def step(k):
            if k == 0:
                give(zl < 3, up[0], own, block(zl), zl + 1)
                give(zl > 0, down[0], own, block(zl), zl - 1)
                return

            @pl.when(zl >= k)
            def _():
                wait(up[k - 1], block(zl - k))

            @pl.when(zl <= 3 - k)
            def _():
                wait(down[k - 1], block(zl + k))

            if k < 3:
                a, b = jnp.maximum(zl - k, 0), jnp.minimum(zl + k, 3)
                give(jnp.logical_and(zl >= k, zl < 3), up[k], block(a), block(a), zl + 1)
                give(jnp.logical_and(zl <= 3 - k, zl > 0), down[k], block(b), block(b), zl - 1)

        return step

    def flush_lines():
        for when, r, dst, zz in maybe:
            @pl.when(when)
            def _():
                copy(r, dst, dst, seq_of(y, zz, c), g).wait_send()

    def flush(upto):
        for one in started[:upto]:
            one.wait_send()
        del started[:upto]

    def wait(r, dst):
        copy(r, dst, dst, seq_of(y, zl, oc), g).wait_recv()

    part_s, part_g = g * 4 + s % 4, s // 4
    same = jnp.logical_and(x == y, zh == zl // 2)
    barrier = pltpu.get_barrier_semaphore()
    peers = [(seq_of(y, (zl + d) % 4, c), g) for d in (1, 2, 3)]
    peers += [(seq_of(y, (zl + d) % 4, c), head_of(x, oh)) for d in (0, 1, 2, 3)]
    peers += [(s, head_of((x + d) % 4, h)) for d in (1, 2, 3) for h in (zh, oh)]
    peers += [(seq_of((y + d) % 4, zl, c), g) for d in (1, 2, 3)]
    peers += [(seq_of(y, (zl + d) % 4, oc), g) for d in (0, 1, 2, 3)]
    for ss, gg in peers:
        pl.semaphore_signal(barrier, inc=1, device_id=(ss, gg), device_id_type=MESH)

    @pl.when(jnp.logical_not(same))
    def _():
        pl.semaphore_signal(barrier, inc=1, device_id=(part_s, part_g), device_id_type=MESH)

    local = [
        (normed, xn.at[g]), (gnormed, gn.at[g]), (gqkv_t, gq.at[:, y, zl, c]),
        (qkv_t, qw), (stream, sb), (gstream, gsb),
    ]
    local = [pltpu.make_async_copy(a, b, local_sem.at[i]) for i, (a, b) in enumerate(local)]
    for one in local:
        one.start()

    token = s * ROWS + lax.broadcasted_iota(jnp.int32, (ROWS, 128), 0)
    for r in range(TOKENS // 128):
        row = layout[pl.ds(r, 1), :]
        hot[:, r * 128 : (r + 1) * 128] = jnp.where(token == row, 1.0, 0.0).astype(BF16)
    fin[...] = fin_t[...].astype(F32).T.astype(BF16)
    for buf in (pg, pm):
        buf[...] = jnp.zeros_like(buf)

    pl.semaphore_wait(barrier, len(peers) + 1 - same.astype(jnp.int32))

    gq_line = line(lambda zz: gq.at[:, y, zz, c], gqkv_t)
    gq_line(0)
    low, high = pl.ds(0, HALF), pl.ds(HALF, HALF)
    whole = pl.ds(0, ROWS)
    sets = [
        (gn, gnormed, whole, low, high), (xn, normed, low, low, None), (xn, normed, high, None, high),
    ]
    r_cross, r_p, r_m, r_rp, r_rm = (
        [[role(), role()] for _ in sets] for _ in range(5)
    )
    for i, (buf, src, rows, _, _) in enumerate(sets):
        send(r_cross[i][0], src.at[rows], buf.at[g, rows], s, head_of(x, oh))
    for i, (buf, src, rows, _, _) in enumerate(sets):
        send(r_p[i][0], src.at[rows], buf.at[g, rows], s, head_of(xp, zh))
        send(r_m[i][0], src.at[rows], buf.at[g, rows], s, head_of(xm, zh))

    moved = [
        (out_t, wt.at[x, zh * 2 + zl % 2, c], wt.at[y, zl, c]),
        (gout_t, gwt.at[x, zh * 2 + zl % 2, c], gwt.at[y, zl, c]),
        (fin, fw.at[zl % 2, c], fw.at[zl % 2, c]),
        (gfin, gfw.at[zl % 2, c], gfw.at[zl % 2, c]),
    ]
    r_perm = [role() for _ in moved]

    @pl.when(jnp.logical_not(same))
    def _():
        for r, (src, there, _) in zip(r_perm, moved):
            copy(r, src, there, part_s, part_g).start()

    @pl.when(same)
    def _():
        for r, (src, _, here) in zip(r_perm, moved):
            pltpu.make_async_copy(src, here, recv_sem.at[r]).start()

    def relay(i, h):
        buf, _, rows, up, down = sets[i]
        k = 0 if h is zh else 1
        from_m, from_p = head_of(xm, h), head_of(xp, h)
        for first in (True, False) if up is not None else (False, True):
            if first:
                wait(r_p[i][k], buf.at[from_m, rows])
                if up is not None:
                    piece = buf.at[from_m, up]
                    send(r_rp[i][k], piece, piece, s, head_of(xp, zh))
            else:
                wait(r_m[i][k], buf.at[from_p, rows])
                if down is not None:
                    piece = buf.at[from_p, down]
                    send(r_rm[i][k], piece, piece, s, head_of(xm, zh))

    def far(i, h):
        buf, _, _, up, down = sets[i]
        k = 0 if h is zh else 1
        if up is not None:
            wait(r_rp[i][k], buf.at[head_of(x2, h), up])
        if down is not None:
            wait(r_rm[i][k], buf.at[head_of(x2, h), down])

    def onward(i):
        buf, _, rows, _, _ = sets[i]
        other = buf.at[head_of(x, oh), rows]
        wait(r_cross[i][0], other)
        send(r_p[i][1], other, other, s, head_of(xp, zh))
        send(r_m[i][1], other, other, s, head_of(xm, zh))

    def project(gg, first=False):
        rows = xn[gg]
        for i in range(3):
            part = jnp.dot(
                rows, qw[i, pl.ds(pl.multiple_of(gg * KC, KC), KC), :], preferred_element_type=F32
            )
            acc[i] = part if first else acc[i] + part

    def gproject(gg, first=False):
        rows = gn[gg]
        for i in range(3):
            block = gq[i, gg // 2, pl.ds((gg % 2) * 2, 2)].reshape(GKC, HD)
            part = jnp.dot(rows, block, preferred_element_type=F32)
            gacc[i] = part if first else gacc[i] + part

    gq_line(1)
    relay(0, zh)
    onward(0)
    gq_line(2)
    relay(1, zh)
    relay(2, zh)
    gq_line(3)
    local[2].wait()
    r_gqy, r_gqc = [role() for _ in range(3)], role()
    mine = gq.at[:, y, :, c]
    for d in (1, 3, 2):
        send(r_gqy[d - 1], mine, mine, seq_of((y + d) % 4, zl, c), g)
    onward(1)
    for i in (0, 1, 3):
        local[i].wait()
    project(g, True)
    project(head_of(xm, zh))
    onward(2)
    for d in (1, 2, 3):
        wait(r_gqy[d - 1], gq.at[:, (y + 4 - d) % 4, :, c])
    send(r_gqc, gq.at[:, :, :, c], gq.at[:, :, :, c], seq_of(y, zl, oc), g)
    for r, (_, _, here) in zip(r_perm, moved):
        wait(r, here)
    w_lines = [line(lambda zz, buf=buf: buf.at[y, zz, c], buf.at[y, zl, c]) for buf in (wt, gwt)]
    for one in w_lines:
        one(0)
    zn = zl + 1 - 2 * (zl % 2)
    r_fz, r_gfz = role(), role()
    send(r_fz, fw.at[zl % 2, c], fw.at[zl % 2, c], seq_of(y, zn, c), g)
    send(r_gfz, gfw.at[zl % 2, c], gfw.at[zl % 2, c], seq_of(y, zn, c), g)
    project(head_of(xp, zh))
    relay(0, oh)
    project(head_of(x, oh))
    for i in range(3):
        far(i, zh)
    relay(1, oh)
    project(head_of(x2, zh))
    relay(2, oh)
    for one in w_lines:
        one(1)
    project(head_of(xm, oh))
    project(head_of(xp, oh))
    wait(r_gqc, gq.at[:, :, :, oc])
    gproject(g, True)
    for gg in (head_of(xm, zh), head_of(xp, zh), head_of(x2, zh), head_of(x, oh)):
        gproject(gg)
    gproject(head_of(xm, oh))
    gproject(head_of(xp, oh))
    far(0, oh)
    gproject(head_of(x2, oh))
    far(1, oh)
    far(2, oh)
    project(head_of(x2, oh))
    for i in range(3):
        for j in range(3):
            packed[i, j] = acc[i, :, j * HD : (j + 1) * HD].astype(BF16)
        packed[i, 3] = gacc[i].astype(BF16)

    sent_a = len(started)

    own = [
        pltpu.make_async_copy(packed.at[0, zl], qb.at[zl], local_sem.at[6]),
        pltpu.make_async_copy(packed.at[1:3, zl], kv.at[:, y, c, zl], local_sem.at[7]),
    ]
    for one in own:
        one.start()
    r_q, r_kv = [role() for _ in range(3)], [role() for _ in range(3)]
    for d in (1, 2, 3):
        j = (zl + d) % 4
        there = seq_of(y, j, c)
        send(r_kv[d - 1], packed.at[1:3, j], kv.at[:, y, c, zl], there, g)
    for d in (1, 2, 3):
        j = (zl + d) % 4
        send(r_q[d - 1], packed.at[0, j], qb.at[zl], seq_of(y, j, c), g)
    for one in w_lines:
        one(2)
    r_kp, r_km = [role() for _ in range(4)], [role() for _ in range(4)]
    r_kc, r_kr = [role() for _ in range(4)], [role() for _ in range(4)]
    r_kcm, r_kcp, r_kc2 = role(), role(), role()
    for d in range(4):
        k = (zl + 4 - d) % 4
        block = kv.at[:, y, c, k]
        if d == 0:
            own[1].wait()
        else:
            wait(r_kv[d - 1], block)
        send(r_kp[d], block, block, seq_of(yp, zl, c), g)
        send(r_km[d], block, block, seq_of(ym, zl, c), g)
        send(r_kr[d], block, block, seq_of(y2, zl, c), g)
        send(r_kc[d], block, block, seq_of(y, zl, oc), g)
    own[0].wait()
    for d in (1, 2, 3):
        wait(r_q[d - 1], qb.at[(zl + 4 - d) % 4])

    def absorb(yy, cc, first=False):
        keys = kv[0, yy, cc].reshape(4 * ROWS, HD)
        values = kv[1, yy, cc].reshape(4 * ROWS, HD)
        queries = qb[...].reshape(4 * ROWS, HD)
        scores = lax.dot_general(keys, queries, NT, preferred_element_type=F32)
        highest = jnp.max(scores, axis=0, keepdims=True)
        if not first:
            before = top[...]
            highest = jnp.maximum(highest, before)
        expd = jnp.exp2((scores - highest) * SCALE2)
        total = jnp.sum(expd, axis=0, keepdims=True)
        mixed = lax.dot_general(values, expd.astype(BF16), TN, preferred_element_type=F32)
        top[...] = highest
        if first:
            tot[...] = total
            ot[...] = mixed
        else:
            shrink = jnp.exp2((before - highest) * SCALE2)
            tot[...] = tot[...] * shrink + total
            ot[...] = ot[...] * shrink + mixed

    absorb(y, c, True)
    for d in range(4):
        wait(r_kc[d], kv.at[:, y, oc, (zl + 4 - d) % 4])
    absorb(y, oc)
    for d in range(4):
        wait(r_kp[d], kv.at[:, ym, c, (zl + 4 - d) % 4])
    send(r_kcm, kv.at[:, ym, c], kv.at[:, ym, c], seq_of(y, zl, oc), g)
    for d in range(4):
        wait(r_km[d], kv.at[:, yp, c, (zl + 4 - d) % 4])
    send(r_kcp, kv.at[:, yp, c], kv.at[:, yp, c], seq_of(y, zl, oc), g)
    for one in w_lines:
        one(3)
    r_w = [[role() for _ in range(6)] for _ in range(2)]
    for r, buf in zip(r_w, (wt, gwt)):
        block = buf.at[y, :, c]
        send(r[0], block, block, seq_of(yp, zl, c), g)
        send(r[1], block, block, seq_of(ym, zl, c), g)
    absorb(ym, c)
    absorb(yp, c)
    for d in range(4):
        wait(r_kr[d], kv.at[:, y2, c, (zl + 4 - d) % 4])
    send(r_kc2, kv.at[:, y2, c], kv.at[:, y2, c], seq_of(y, zl, oc), g)
    wait(r_kcm, kv.at[:, ym, oc])
    absorb(ym, oc)
    wait(r_kcp, kv.at[:, yp, oc])
    absorb(yp, oc)
    absorb(y2, c)
    wait(r_fz, fw.at[1 - zl % 2, c])
    wait(r_gfz, gfw.at[1 - zl % 2, c])
    r_fc, r_gfc = role(), role()
    send(r_fc, fw.at[:, c], fw.at[:, c], seq_of(y, zl, oc), g)
    send(r_gfc, gfw.at[:, c], gfw.at[:, c], seq_of(y, zl, oc), g)
    flush(sent_a)
    wait(r_kc2, kv.at[:, y2, oc])
    absorb(y2, oc)
    ob[...] = (ot[...] / tot[...]).T.astype(BF16)

    r_o = [[role(), role()] for _ in range(4)]
    for d in (0, 1, 2, 3):
        k = (zl + d) % 4
        block = ob.at[pl.ds(pl.multiple_of(k * ROWS, ROWS), ROWS), :]
        for e, h in enumerate((zh, oh)):
            if d == 0 and e == 0:
                pltpu.make_async_copy(block, at.at[x, zh, zl], recv_sem.at[r_o[0][0]]).start()
            else:
                send(r_o[d][e], block, at.at[x, zh, zl], seq_of(y, k, c), head_of(x, h))
    first_o = r_o[0][0]

    def column_sums(gains, weights, width, keep):
        n = width // 128
        row = jnp.concatenate([gains[pl.ds(g * n + i, 1), :] for i in range(n)], axis=1)
        rest = row - row.astype(BF16).astype(F32)
        at_row = lax.broadcasted_iota(jnp.int32, (16, width), 0)
        both = jnp.where(at_row == 0, row, jnp.where(at_row == 1, rest, 0.0)).astype(BF16)
        sums = jnp.dot(both, weights[...].reshape(width, 64), preferred_element_type=F32)
        sums = jnp.broadcast_to(jnp.sum(sums, axis=0, keepdims=True), (64, 64)).T
        for i in range(8):
            keep[i, 0:8, ROWS:] = sums[i * 8 : (i + 1) * 8]

    wait(r_fc, fw.at[:, oc])
    wait(r_gfc, gfw.at[:, oc])
    column_sums(ggain, gfw, GKC, pg)
    column_sums(gain, fw, KC, pm)

    def arrived(j):
        d = (zl + 4 - j) % 4
        for e, h in enumerate((zh, oh)):
            wait(first_o + d * 2 + e, at.at[x, h, j])

    r_gx = [role() for _ in range(4)]
    r_mx = [role() for _ in range(4)]
    arrived(3)
    send(r_gx[0], at.at[x, :, 3], at.at[x, :, 3], s, head_of(xp, zh))
    send(r_gx[1], at.at[x, :, 3], at.at[x, :, 3], s, head_of(xm, zh))
    for j in range(3):
        arrived(j)
    send(r_mx[0], at.at[x, :, 0:3], at.at[x, :, 0:3], s, head_of(xp, zh))
    send(r_mx[1], at.at[x, :, 0:3], at.at[x, :, 0:3], s, head_of(xm, zh))

    for r, buf in zip(r_w, (wt, gwt)):
        a, b = buf.at[ym, 0:2, c], buf.at[yp, 2:4, c]
        wait(r[0], buf.at[ym, :, c])
        send(r[2], a, a, seq_of(yp, zl, c), g)
        wait(r[1], buf.at[yp, :, c])
        send(r[3], b, b, seq_of(ym, zl, c), g)
    wait(r_gx[0], at.at[xm, :, 3])
    send(r_gx[2], at.at[xm, 0, 3], at.at[xm, 0, 3], s, head_of(xp, zh))
    wait(r_gx[1], at.at[xp, :, 3])
    send(r_gx[3], at.at[xp, 1, 3], at.at[xp, 1, 3], s, head_of(xm, zh))
    wait(r_mx[0], at.at[xm, :, 0:3])
    send(r_mx[2], at.at[xm, 0, 0:3], at.at[xm, 0, 0:3], s, head_of(xp, zh))
    wait(r_mx[1], at.at[xp, :, 0:3])
    send(r_mx[3], at.at[xp, 1, 0:3], at.at[xp, 1, 0:3], s, head_of(xm, zh))
    for r, buf in zip(r_w, (wt, gwt)):
        wait(r[2], buf.at[y2, 0:2, c])
        wait(r[3], buf.at[y2, 2:4, c])
        send(r[4], buf.at[:, :, c], buf.at[:, :, c], seq_of(y, zl, oc), g)
    local[4].wait()
    local[5].wait()

    def gout_part(xx):
        total = None
        for h in range(2):
            block = gwt[xx, h * 2 : h * 2 + 2].reshape(GKC, HD)
            part = lax.dot_general(at[xx, h, 3], block, NT, preferred_element_type=F32)
            total = part if total is None else total + part
        return total

    def out_part(xx):
        total = None
        for h in range(2):
            rows = jnp.concatenate([at[xx, h, j] for j in range(3)], axis=1)
            block = wt[xx, h * 2 : h * 2 + 2].reshape(KC, 3 * HD)
            part = lax.dot_general(rows, block, NT, preferred_element_type=F32)
            total = part if total is None else total + part
        return total

    def spread(ref, width, gains, weights, keep, buf, roles):
        one = jnp.zeros((ROWS, 128), F32)
        two = jnp.zeros((ROWS, 128), F32)
        for i in range(width // 128):
            cols = ref[:, i * 128 : (i + 1) * 128]
            one = one + cols
            two = two + cols * cols
        center = jnp.sum(one, axis=1, keepdims=True) * (1.0 / width)
        parts = []
        for i in range(width // 128):
            row = gains[pl.ds(g * (width // 128) + i, 1), :]
            parts.append(((ref[:, i * 128 : (i + 1) * 128] - center) * row).astype(BF16))
        part = jnp.dot(
            jnp.concatenate(parts, axis=1), weights[...].reshape(width, 64),
            preferred_element_type=F32,
        ).T
        one = jnp.sum(one.T, axis=0, keepdims=True)
        two = jnp.sum(two.T, axis=0, keepdims=True)
        for i in range(8):
            keep[i, 0:8, 0:ROWS] = part[i * 8 : (i + 1) * 8]
            keep[i, 8:9, 0:ROWS] = one
            keep[i, 9:10, 0:ROWS] = two
        for d in range(1, 8):
            k = (g + d) % 8
            send(roles[d - 1], keep.at[k], buf.at[g], s, k)
        buf[g] = keep[g]

    def combine(width, buf, roles):
        for d in range(1, 8):
            wait(roles[d - 1], buf.at[(g + 8 - d) % 8])
        one, two = buf[0, 8:9, 0:ROWS], buf[0, 9:10, 0:ROWS]
        for i in range(1, 8):
            one, two = one + buf[i, 8:9, 0:ROWS], two + buf[i, 9:10, 0:ROWS]
        center, square = one * (0.125 / width), two * (0.125 / width)
        scale = lax.rsqrt(square - center * center + EPS)
        total = jnp.zeros((8, ROWS), F32)
        for i in range(8):
            shift = buf[i, 8:9, 0:ROWS] * (1.0 / width) - center
            total = total + (buf[i, 0:8, 0:ROWS] + shift * buf[i, 0:8, ROWS : ROWS + 1])
        return total * scale

    r_pg, r_pm, r_out = ([role() for _ in range(7)] for _ in range(3))
    sent_d = len(started)
    wait(r_w[1][4], gwt.at[:, :, oc])
    ghid[...] = gsb[...].astype(F32) + gout_part(x)
    ghid[...] += gout_part(xm)
    ghid[...] += gout_part(xp)
    wait(r_gx[2], at.at[x2, 0, 3])
    wait(r_gx[3], at.at[x2, 1, 3])
    ghid[...] += gout_part(x2)
    spread(ghid, GKC, ggain, gfw, pg, rg, r_pg)
    wait(r_w[0][4], wt.at[:, :, oc])
    hid[...] = sb[...].astype(F32) + out_part(x)
    hid[...] += out_part(xm)
    hid[...] += out_part(xp)
    wait(r_mx[2], at.at[x2, 0, 0:3])
    wait(r_mx[3], at.at[x2, 1, 0:3])
    hid[...] += out_part(x2)
    spread(hid, KC, gain, fw, pm, rm, r_pm)
    gp[y, zl, c] = combine(GKC, rg, r_pg)
    near = [(d, e) for d in range(4) for e in range(2) if d or e]
    r_az, r_ay = [role() for _ in near], [role() for _ in range(3)]
    for r, (d, e) in zip(r_az, near):
        block = gp.at[y, zl, c]
        send(r, block, block, seq_of(y, (zl + d) % 4, oc if e else c), g)
    flush(sent_d)
    flush_lines()

    @pl.when(jnp.logical_not(same))
    def _():
        for r, (src, there, _) in zip(r_perm, moved):
            copy(r, src, there, part_s, part_g).wait_send()

    for r, (d, e) in zip(r_az, near):
        wait(r, gp.at[y, (zl + 4 - d) % 4, oc if e else c])
    for d in (1, 2, 3):
        send(r_ay[d - 1], gp.at[y], gp.at[y], seq_of((y + d) % 4, zl, c), g)
    main_pred = combine(KC, rm, r_pm)
    for d in (1, 2, 3):
        wait(r_ay[d - 1], gp.at[(y + 4 - d) % 4])

    lane = lax.broadcasted_iota(jnp.int32, (8, 128), 1)
    pieces = []
    for yy in range(4):
        for zz in range(4):
            a0, a1 = gp[yy, zz, 0, :, 0:128], gp[yy, zz, 0, :, 128:192]
            b0, b1 = gp[yy, zz, 1, :, 0:64], gp[yy, zz, 1, :, 64:192]
            pieces += [a0, jnp.concatenate([a1, b0], axis=1), b1]
    slots = jnp.concatenate(pieces, axis=1)
    upper = slots.astype(BF16)
    lower = (slots - upper.astype(F32)).astype(BF16)
    both = jnp.concatenate([upper, lower], axis=0)
    picked = lax.dot_general(both, hot[...], NT, preferred_element_type=F32)
    picked = picked[0:8] + picked[8:16]

    first = s * ROWS
    frame = first // FRAME_TOK
    last = (first + ROWS - 1) // FRAME_TOK
    owned = first + lax.broadcasted_iota(jnp.int32, (8, ROWS), 1)
    strength = 1.0 + jnp.where(owned // FRAME_TOK == frame, flags[frame], flags[last]).astype(F32)
    outb[g] = picked + strength * (main_pred - picked)
    for d in range(1, 8):
        send(r_out[d - 1], outb.at[g], outb.at[g], s, (g + d) % 8)
    flush(len(started) - 7)
    for d in range(1, 8):
        wait(r_out[d - 1], outb.at[(g + 8 - d) % 8])
    for i in range(8):
        out[i * 8 : (i + 1) * 8, :] = outb[i]

    flush(len(started))


def per_device(
    stream, normed, qkv_weight, out_weight, final_gain, final_weight, guide_stream, guide_normed,
    guide_qkv, guide_out, guide_gain, guide_final, layout, flags,
):
    anyw = pl.BlockSpec(memory_space=pl.ANY)
    vmem = pl.BlockSpec(memory_space=pltpu.VMEM)
    smem = pl.BlockSpec(memory_space=pltpu.SMEM)
    v = pltpu.VMEM
    scratch = [
        v((8, ROWS, KC), BF16),
        v((8, ROWS, GKC), BF16),
        v((3, 5120, 384), BF16),
        v((3, 4, 4, 2, 64, HD), BF16),
        v((4, 4, 2, 160, 384), BF16),
        v((4, 4, 2, 64, HD), BF16),
        v((2, 2, 160, 64), BF16),
        v((2, 2, 64, 64), BF16),
        v((ROWS, KC), BF16),
        v((ROWS, GKC), BF16),
        v((3, ROWS, 384), F32),
        v((3, ROWS, HD), F32),
        v((3, 4, ROWS, HD), BF16),
        v((4, ROWS, HD), BF16),
        v((2, 4, 2, 4, ROWS, HD), BF16),
        v((1, 4 * ROWS), F32),
        v((1, 4 * ROWS), F32),
        v((HD, 4 * ROWS), F32),
        v((4 * ROWS, HD), BF16),
        v((4, 2, 4, ROWS, HD), BF16),
        v((ROWS, TOKENS), BF16),
        v((ROWS, KC), F32),
        v((ROWS, GKC), F32),
        v((160, 64), BF16),
        v((8, 16, 256), F32),
        v((8, 16, 256), F32),
        v((8, 16, 256), F32),
        v((8, 16, 256), F32),
        v((4, 4, 2, 8, ROWS), F32),
        v((8, 8, ROWS), F32),
        pltpu.SemaphoreType.DMA((192,)),
        pltpu.SemaphoreType.DMA((192,)),
        pltpu.SemaphoreType.DMA((8,)),
    ]
    guided = pl.pallas_call(
        body,
        out_shape=jax.ShapeDtypeStruct((64, ROWS), F32),
        in_specs=[anyw] * 4 + [vmem, vmem] + [anyw] * 4 + [vmem, anyw, vmem, smem],
        out_specs=vmem,
        scratch_shapes=scratch,
        compiler_params=pltpu.CompilerParams(
            collective_id=0, has_side_effects=True, vmem_limit_bytes=56 * 1024 * 1024
        ),
        cost_estimate=pl.CostEstimate(
            flops=6_000_000_000, bytes_accessed=20_000_000, transcendentals=5_000_000
        ),
    )(
        stream, normed, jnp.transpose(qkv_weight, (1, 0, 2)), out_weight.T,
        final_gain.reshape(40, 128), final_weight.T, guide_stream, guide_normed,
        jnp.transpose(guide_qkv, (1, 0, 2)), guide_out.T, guide_gain.reshape(16, 128), guide_final,
        layout.reshape(48, 128), flags,
    )
    return guided.T


def solution(mesh):
    placed = (
        P("seq", "head"),
        P("seq", "head"),
        P(None, None, "head"),
        P("head", "seq"),
        P(),
        P("seq", None),
        P("seq", "head"),
        P("seq", "head"),
        P("seq", None, "head"),
        P("head", "seq"),
        P(),
        P("seq", None),
        P(),
        P(),
    )
    return jax.shard_map(
        per_device, mesh=mesh, in_specs=placed, out_specs=P("seq", None), check_vma=False
    )
```

```python
import math

import jax
import jax.numpy as jnp
from jax import lax
from jax.experimental import pallas as pl
from jax.experimental.pallas import tpu as pltpu
from jax.sharding import PartitionSpec as P

HD = 128
FRAME_TOK = 512
EPS = 1e-05
TEMPER = 2.5
SCALE2 = TEMPER / math.sqrt(HD) * math.log2(math.e)
F32, BF16 = jnp.float32, jnp.bfloat16
MESH = pl.DeviceIdType.MESH

ROWS = 192
HALF = 96
KC, GKC = 640, 256
TOKENS = 6144
NT = (((1,), (1,)), ((), ()))
TN = (((0,), (0,)), ((), ()))


def body(
    stream, normed, qkv_t, out_t, gain, fin_t, gstream, gnormed, gqkv_t, gout_t, ggain, gfin,
    layout, flags, out,
    xn, gn, qw, gq, wt, gwt, fw, gfw, sb, gsb, acc, gacc, packed, qb, kv, top, tot, ot, ob, at,
    hot, hid, ghid, fin, pg, pm, rg, rm, gp, outb,
    send_sem, recv_sem, local_sem,
):
    s, g = lax.axis_index("seq"), lax.axis_index("head")
    y, zl, c = s // 8, (s // 2) % 4, s % 2
    x, zh = g // 2, g % 2

    def seq_of(yy, zz, cc):
        return yy * 8 + zz * 2 + cc

    def head_of(xx, hh):
        return xx * 2 + hh

    xp, xm, x2 = (x + 1) % 4, (x + 3) % 4, (x + 2) % 4
    yp, ym, y2 = (y + 1) % 4, (y + 3) % 4, (y + 2) % 4
    oc, oh = 1 - c, 1 - zh
    started = []
    count = [0]

    def role():
        count[0] += 1
        return count[0] - 1

    def copy(r, src, dst, ss, gg):
        return pltpu.make_async_remote_copy(
            src_ref=src, dst_ref=dst, send_sem=send_sem.at[r], recv_sem=recv_sem.at[r],
            device_id=(ss, gg), device_id_type=MESH,
        )

    def send(r, src, dst, ss, gg):
        one = copy(r, src, dst, ss, gg)
        one.start()
        started.append(one)

    def flush(upto):
        for one in started[:upto]:
            one.wait_send()
        del started[:upto]

    def wait(r, dst):
        copy(r, dst, dst, seq_of(y, zl, oc), g).wait_recv()

    part_s, part_g = g * 4 + s % 4, s // 4
    same = jnp.logical_and(x == y, zh == zl // 2)
    barrier = pltpu.get_barrier_semaphore()
    peers = [(seq_of(y, (zl + d) % 4, c), g) for d in (1, 2, 3)]
    peers += [(seq_of(y, (zl + d) % 4, c), head_of(x, oh)) for d in (0, 1, 2, 3)]
    peers += [(s, head_of((x + d) % 4, h)) for d in (1, 2, 3) for h in (zh, oh)]
    peers += [(seq_of((y + d) % 4, zl, c), g) for d in (1, 2, 3)]
    peers += [(seq_of(y, (zl + d) % 4, oc), g) for d in (0, 1, 2, 3)]
    for ss, gg in peers:
        pl.semaphore_signal(barrier, inc=1, device_id=(ss, gg), device_id_type=MESH)

    @pl.when(jnp.logical_not(same))
    def _():
        pl.semaphore_signal(barrier, inc=1, device_id=(part_s, part_g), device_id_type=MESH)

    local = [
        (normed, xn.at[g]), (gnormed, gn.at[g]), (gqkv_t, gq.at[:, y, zl, c]),
        (qkv_t, qw), (stream, sb), (gstream, gsb),
    ]
    local = [pltpu.make_async_copy(a, b, local_sem.at[i]) for i, (a, b) in enumerate(local)]
    for one in local:
        one.start()

    token = s * ROWS + lax.broadcasted_iota(jnp.int32, (ROWS, 128), 0)
    for r in range(TOKENS // 128):
        row = layout[pl.ds(r, 1), :]
        hot[:, r * 128 : (r + 1) * 128] = jnp.where(token == row, 1.0, 0.0).astype(BF16)
    fin[...] = fin_t[...].astype(F32).T.astype(BF16)
    for buf in (pg, pm):
        buf[...] = jnp.zeros_like(buf)

    pl.semaphore_wait(barrier, len(peers) + 1 - same.astype(jnp.int32))

    low, high = pl.ds(0, HALF), pl.ds(HALF, HALF)
    whole = pl.ds(0, ROWS)
    sets = [
        (gn, gnormed, whole, low, high), (xn, normed, low, low, None), (xn, normed, high, None, high),
    ]
    r_cross, r_p, r_m, r_rp, r_rm = (
        [[role(), role()] for _ in sets] for _ in range(5)
    )
    for i, (buf, src, rows, _, _) in enumerate(sets):
        send(r_cross[i][0], src.at[rows], buf.at[g, rows], s, head_of(x, oh))
    for i, (buf, src, rows, _, _) in enumerate(sets):
        send(r_p[i][0], src.at[rows], buf.at[g, rows], s, head_of(xp, zh))
        send(r_m[i][0], src.at[rows], buf.at[g, rows], s, head_of(xm, zh))

    moved = [
        (out_t, wt.at[x, zh * 2 + zl % 2, c], wt.at[y, zl, c]),
        (gout_t, gwt.at[x, zh * 2 + zl % 2, c], gwt.at[y, zl, c]),
        (fin, fw.at[zl % 2, c], fw.at[zl % 2, c]),
        (gfin, gfw.at[zl % 2, c], gfw.at[zl % 2, c]),
    ]
    r_perm = [role() for _ in moved]

    @pl.when(jnp.logical_not(same))
    def _():
        for r, (src, there, _) in zip(r_perm, moved):
            copy(r, src, there, part_s, part_g).start()

    @pl.when(same)
    def _():
        for r, (src, _, here) in zip(r_perm, moved):
            pltpu.make_async_copy(src, here, recv_sem.at[r]).start()

    def relay(i, h):
        buf, _, rows, up, down = sets[i]
        k = 0 if h is zh else 1
        from_m, from_p = head_of(xm, h), head_of(xp, h)
        for first in (True, False) if up is not None else (False, True):
            if first:
                wait(r_p[i][k], buf.at[from_m, rows])
                if up is not None:
                    piece = buf.at[from_m, up]
                    send(r_rp[i][k], piece, piece, s, head_of(xp, zh))
            else:
                wait(r_m[i][k], buf.at[from_p, rows])
                if down is not None:
                    piece = buf.at[from_p, down]
                    send(r_rm[i][k], piece, piece, s, head_of(xm, zh))

    def far(i, h):
        buf, _, _, up, down = sets[i]
        k = 0 if h is zh else 1
        if up is not None:
            wait(r_rp[i][k], buf.at[head_of(x2, h), up])
        if down is not None:
            wait(r_rm[i][k], buf.at[head_of(x2, h), down])

    def onward(i):
        buf, _, rows, _, _ = sets[i]
        other = buf.at[head_of(x, oh), rows]
        wait(r_cross[i][0], other)
        send(r_p[i][1], other, other, s, head_of(xp, zh))
        send(r_m[i][1], other, other, s, head_of(xm, zh))

    def project(gg, first=False):
        rows = xn[gg]
        for i in range(3):
            part = jnp.dot(
                rows, qw[i, pl.ds(pl.multiple_of(gg * KC, KC), KC), :], preferred_element_type=F32
            )
            acc[i] = part if first else acc[i] + part

    def gproject(gg, first=False):
        rows = gn[gg]
        for i in range(3):
            block = gq[i, gg // 2, pl.ds((gg % 2) * 2, 2)].reshape(GKC, HD)
            part = jnp.dot(rows, block, preferred_element_type=F32)
            gacc[i] = part if first else gacc[i] + part

    relay(0, zh)
    onward(0)
    relay(1, zh)
    relay(2, zh)
    onward(1)
    for i in (0, 1, 3):
        local[i].wait()
    project(g, True)
    project(head_of(xm, zh))
    onward(2)
    r_gqz = [role() for _ in range(3)]
    for d in (1, 2, 3):
        send(r_gqz[d - 1], gqkv_t, gq.at[:, y, zl, c], seq_of(y, (zl + d) % 4, c), g)
    project(head_of(xp, zh))
    relay(0, oh)
    project(head_of(x, oh))
    for i in range(3):
        far(i, zh)
    relay(1, oh)
    project(head_of(x2, zh))
    relay(2, oh)
    local[2].wait()
    for d in (1, 2, 3):
        wait(r_gqz[d - 1], gq.at[:, y, (zl + 4 - d) % 4, c])
    r_gqy, r_gqc = [role() for _ in range(3)], role()
    mine = gq.at[:, y, :, c]
    for d in (1, 3, 2):
        send(r_gqy[d - 1], mine, mine, seq_of((y + d) % 4, zl, c), g)
    project(head_of(xm, oh))
    project(head_of(xp, oh))
    far(1, oh)
    far(2, oh)
    project(head_of(x2, oh))
    for i in range(3):
        for j in range(3):
            packed[i, j] = acc[i, :, j * HD : (j + 1) * HD].astype(BF16)
    sent_a = len(started)

    r_q, r_kv = [role() for _ in range(3)], [role() for _ in range(3)]

    def heads(guide):
        for d in (1, 2, 3):
            j = (zl + d) % 4
            there = seq_of(y, j, c)
            both = [
                copy(r_kv[d - 1], packed.at[1:3, j], kv.at[:, y, c, zl], there, g),
                copy(r_q[d - 1], packed.at[0, j], qb.at[zl], there, g),
            ]

            @pl.when(j == 3 if guide else j != 3)
            def _():
                for one in both:
                    one.start()

            if guide:
                started.extend(both)

    heads(False)
    for d in (1, 2, 3):
        wait(r_gqy[d - 1], gq.at[:, (y + 4 - d) % 4, :, c])
    send(r_gqc, gq.at[:, :, :, c], gq.at[:, :, :, c], seq_of(y, zl, oc), g)
    wait(r_gqc, gq.at[:, :, :, oc])
    gproject(g, True)
    for gg in (head_of(xm, zh), head_of(xp, zh), head_of(x2, zh), head_of(x, oh)):
        gproject(gg)
    gproject(head_of(xm, oh))
    gproject(head_of(xp, oh))
    far(0, oh)
    gproject(head_of(x2, oh))
    for i in range(3):
        packed[i, 3] = gacc[i].astype(BF16)
    heads(True)
    own = [
        pltpu.make_async_copy(packed.at[0, zl], qb.at[zl], local_sem.at[6]),
        pltpu.make_async_copy(packed.at[1:3, zl], kv.at[:, y, c, zl], local_sem.at[7]),
    ]
    for one in own:
        one.start()
    for r, (_, _, here) in zip(r_perm, moved):
        wait(r, here)
    r_wz, r_gwz = [role() for _ in range(3)], [role() for _ in range(3)]
    for d in (1, 2, 3):
        there = seq_of(y, (zl + d) % 4, c)
        send(r_wz[d - 1], wt.at[y, zl, c], wt.at[y, zl, c], there, g)
        send(r_gwz[d - 1], gwt.at[y, zl, c], gwt.at[y, zl, c], there, g)
    zn = zl + 1 - 2 * (zl % 2)
    r_fz, r_gfz = role(), role()
    send(r_fz, fw.at[zl % 2, c], fw.at[zl % 2, c], seq_of(y, zn, c), g)
    send(r_gfz, gfw.at[zl % 2, c], gfw.at[zl % 2, c], seq_of(y, zn, c), g)
    r_kp, r_km = [role() for _ in range(4)], [role() for _ in range(4)]
    r_kc, r_kr = [role() for _ in range(4)], [role() for _ in range(4)]
    r_kcm, r_kcp, r_kc2 = role(), role(), role()
    for d in range(4):
        k = (zl + 4 - d) % 4
        block = kv.at[:, y, c, k]
        if d == 0:
            own[1].wait()
        else:
            wait(r_kv[d - 1], block)
        send(r_kp[d], block, block, seq_of(yp, zl, c), g)
        send(r_km[d], block, block, seq_of(ym, zl, c), g)
        send(r_kc[d], block, block, seq_of(y, zl, oc), g)
    own[0].wait()
    for d in (1, 2, 3):
        wait(r_q[d - 1], qb.at[(zl + 4 - d) % 4])

    def absorb(yy, cc, first=False):
        keys = kv[0, yy, cc].reshape(4 * ROWS, HD)
        values = kv[1, yy, cc].reshape(4 * ROWS, HD)
        queries = qb[...].reshape(4 * ROWS, HD)
        scores = lax.dot_general(keys, queries, NT, preferred_element_type=F32)
        highest = jnp.max(scores, axis=0, keepdims=True)
        if not first:
            before = top[...]
            highest = jnp.maximum(highest, before)
        expd = jnp.exp2((scores - highest) * SCALE2)
        total = jnp.sum(expd, axis=0, keepdims=True)
        mixed = lax.dot_general(values, expd.astype(BF16), TN, preferred_element_type=F32)
        top[...] = highest
        if first:
            tot[...] = total
            ot[...] = mixed
        else:
            shrink = jnp.exp2((before - highest) * SCALE2)
            tot[...] = tot[...] * shrink + total
            ot[...] = ot[...] * shrink + mixed

    absorb(y, c, True)
    for d in (0, 1):
        k = (zl + 4 - d) % 4
        wait(r_kp[d], kv.at[:, ym, c, k])
        send(r_kr[d], kv.at[:, ym, c, k], kv.at[:, ym, c, k], seq_of(yp, zl, c), g)
    for d in (2, 3):
        k = (zl + 4 - d) % 4
        wait(r_km[d], kv.at[:, yp, c, k])
        send(r_kr[d], kv.at[:, yp, c, k], kv.at[:, yp, c, k], seq_of(ym, zl, c), g)
    for d in (2, 3):
        wait(r_kp[d], kv.at[:, ym, c, (zl + 4 - d) % 4])
    send(r_kcm, kv.at[:, ym, c], kv.at[:, ym, c], seq_of(y, zl, oc), g)
    for d in (0, 1):
        wait(r_km[d], kv.at[:, yp, c, (zl + 4 - d) % 4])
    send(r_kcp, kv.at[:, yp, c], kv.at[:, yp, c], seq_of(y, zl, oc), g)
    for d in range(4):
        wait(r_kc[d], kv.at[:, y, oc, (zl + 4 - d) % 4])
    absorb(y, oc)
    absorb(ym, c)
    absorb(yp, c)
    for d in range(4):
        wait(r_kr[d], kv.at[:, y2, c, (zl + 4 - d) % 4])
    send(r_kc2, kv.at[:, y2, c], kv.at[:, y2, c], seq_of(y, zl, oc), g)
    for d in (1, 2, 3):
        wait(r_wz[d - 1], wt.at[y, (zl + 4 - d) % 4, c])
        wait(r_gwz[d - 1], gwt.at[y, (zl + 4 - d) % 4, c])
    r_w = [[role() for _ in range(6)] for _ in range(2)]
    for r, buf in ((r_w[1], gwt), (r_w[0], wt)):
        block = buf.at[y, :, c]
        send(r[0], block, block, seq_of(yp, zl, c), g)
        send(r[1], block, block, seq_of(ym, zl, c), g)
    wait(r_kcm, kv.at[:, ym, oc])
    absorb(ym, oc)
    wait(r_kcp, kv.at[:, yp, oc])
    absorb(yp, oc)
    absorb(y2, c)
    wait(r_fz, fw.at[1 - zl % 2, c])
    wait(r_gfz, gfw.at[1 - zl % 2, c])
    r_fc, r_gfc = role(), role()
    send(r_fc, fw.at[:, c], fw.at[:, c], seq_of(y, zl, oc), g)
    send(r_gfc, gfw.at[:, c], gfw.at[:, c], seq_of(y, zl, oc), g)
    flush(sent_a)
    wait(r_kc2, kv.at[:, y2, oc])
    absorb(y2, oc)
    ob[...] = (ot[...] / tot[...]).T.astype(BF16)

    r_o = [[role(), role()] for _ in range(4)]
    for d in (0, 1, 2, 3):
        k = (zl + d) % 4
        block = ob.at[pl.ds(pl.multiple_of(k * ROWS, ROWS), ROWS), :]
        for e, h in enumerate((zh, oh)):
            if d == 0 and e == 0:
                pltpu.make_async_copy(block, at.at[x, zh, zl], recv_sem.at[r_o[0][0]]).start()
            else:
                send(r_o[d][e], block, at.at[x, zh, zl], seq_of(y, k, c), head_of(x, h))
    first_o = r_o[0][0]

    def column_sums(gains, weights, width, keep):
        n = width // 128
        row = jnp.concatenate([gains[pl.ds(g * n + i, 1), :] for i in range(n)], axis=1)
        rest = row - row.astype(BF16).astype(F32)
        at_row = lax.broadcasted_iota(jnp.int32, (16, width), 0)
        both = jnp.where(at_row == 0, row, jnp.where(at_row == 1, rest, 0.0)).astype(BF16)
        sums = jnp.dot(both, weights[...].reshape(width, 64), preferred_element_type=F32)
        sums = jnp.broadcast_to(jnp.sum(sums, axis=0, keepdims=True), (64, 64)).T
        for i in range(8):
            keep[i, 0:8, ROWS:] = sums[i * 8 : (i + 1) * 8]

    wait(r_fc, fw.at[:, oc])
    wait(r_gfc, gfw.at[:, oc])
    column_sums(ggain, gfw, GKC, pg)
    column_sums(gain, fw, KC, pm)

    def arrived(j):
        d = (zl + 4 - j) % 4
        for e, h in enumerate((zh, oh)):
            wait(first_o + d * 2 + e, at.at[x, h, j])

    r_gx = [role() for _ in range(4)]
    r_mx = [role() for _ in range(4)]
    arrived(3)
    send(r_gx[0], at.at[x, :, 3], at.at[x, :, 3], s, head_of(xp, zh))
    send(r_gx[1], at.at[x, :, 3], at.at[x, :, 3], s, head_of(xm, zh))
    for j in range(3):
        arrived(j)
    send(r_mx[0], at.at[x, :, 0:3], at.at[x, :, 0:3], s, head_of(xp, zh))
    send(r_mx[1], at.at[x, :, 0:3], at.at[x, :, 0:3], s, head_of(xm, zh))

    for r, buf in ((r_w[1], gwt), (r_w[0], wt)):
        a, b = buf.at[ym, 0:2, c], buf.at[yp, 2:4, c]
        wait(r[0], buf.at[ym, :, c])
        send(r[2], a, a, seq_of(yp, zl, c), g)
        wait(r[1], buf.at[yp, :, c])
        send(r[3], b, b, seq_of(ym, zl, c), g)
    wait(r_gx[0], at.at[xm, :, 3])
    send(r_gx[2], at.at[xm, 0, 3], at.at[xm, 0, 3], s, head_of(xp, zh))
    wait(r_gx[1], at.at[xp, :, 3])
    send(r_gx[3], at.at[xp, 1, 3], at.at[xp, 1, 3], s, head_of(xm, zh))
    wait(r_mx[0], at.at[xm, :, 0:3])
    send(r_mx[2], at.at[xm, 0, 0:3], at.at[xm, 0, 0:3], s, head_of(xp, zh))
    wait(r_mx[1], at.at[xp, :, 0:3])
    send(r_mx[3], at.at[xp, 1, 0:3], at.at[xp, 1, 0:3], s, head_of(xm, zh))
    for r, buf in ((r_w[1], gwt), (r_w[0], wt)):
        wait(r[2], buf.at[y2, 0:2, c])
        wait(r[3], buf.at[y2, 2:4, c])
        send(r[4], buf.at[:, :, c], buf.at[:, :, c], seq_of(y, zl, oc), g)
    local[4].wait()
    local[5].wait()

    def gout_part(xx):
        total = None
        for h in range(2):
            block = gwt[xx, h * 2 : h * 2 + 2].reshape(GKC, HD)
            part = lax.dot_general(at[xx, h, 3], block, NT, preferred_element_type=F32)
            total = part if total is None else total + part
        return total

    def out_part(xx):
        total = None
        for h in range(2):
            rows = jnp.concatenate([at[xx, h, j] for j in range(3)], axis=1)
            block = wt[xx, h * 2 : h * 2 + 2].reshape(KC, 3 * HD)
            part = lax.dot_general(rows, block, NT, preferred_element_type=F32)
            total = part if total is None else total + part
        return total

    def spread(ref, width, gains, weights, keep, buf, roles):
        one = jnp.zeros((ROWS, 128), F32)
        two = jnp.zeros((ROWS, 128), F32)
        for i in range(width // 128):
            cols = ref[:, i * 128 : (i + 1) * 128]
            one = one + cols
            two = two + cols * cols
        center = jnp.sum(one, axis=1, keepdims=True) * (1.0 / width)
        parts = []
        for i in range(width // 128):
            row = gains[pl.ds(g * (width // 128) + i, 1), :]
            parts.append(((ref[:, i * 128 : (i + 1) * 128] - center) * row).astype(BF16))
        part = jnp.dot(
            jnp.concatenate(parts, axis=1), weights[...].reshape(width, 64),
            preferred_element_type=F32,
        ).T
        one = jnp.sum(one.T, axis=0, keepdims=True)
        two = jnp.sum(two.T, axis=0, keepdims=True)
        for i in range(8):
            keep[i, 0:8, 0:ROWS] = part[i * 8 : (i + 1) * 8]
            keep[i, 8:9, 0:ROWS] = one
            keep[i, 9:10, 0:ROWS] = two
        for d in range(1, 8):
            k = (g + d) % 8
            send(roles[d - 1], keep.at[k], buf.at[g], s, k)
        buf[g] = keep[g]

    def combine(width, buf, roles):
        for d in range(1, 8):
            wait(roles[d - 1], buf.at[(g + 8 - d) % 8])
        one, two = buf[0, 8:9, 0:ROWS], buf[0, 9:10, 0:ROWS]
        for i in range(1, 8):
            one, two = one + buf[i, 8:9, 0:ROWS], two + buf[i, 9:10, 0:ROWS]
        center, square = one * (0.125 / width), two * (0.125 / width)
        scale = lax.rsqrt(square - center * center + EPS)
        total = jnp.zeros((8, ROWS), F32)
        for i in range(8):
            shift = buf[i, 8:9, 0:ROWS] * (1.0 / width) - center
            total = total + (buf[i, 0:8, 0:ROWS] + shift * buf[i, 0:8, ROWS : ROWS + 1])
        return total * scale

    r_pg, r_pm, r_out = ([role() for _ in range(7)] for _ in range(3))
    sent_d = len(started)
    wait(r_w[1][4], gwt.at[:, :, oc])
    ghid[...] = gsb[...].astype(F32) + gout_part(x)
    ghid[...] += gout_part(xm)
    ghid[...] += gout_part(xp)
    wait(r_gx[2], at.at[x2, 0, 3])
    wait(r_gx[3], at.at[x2, 1, 3])
    ghid[...] += gout_part(x2)
    spread(ghid, GKC, ggain, gfw, pg, rg, r_pg)
    gp[y, zl, c] = combine(GKC, rg, r_pg)
    near = [(d, e) for d in range(4) for e in range(2) if d or e]
    r_az, r_ay = [role() for _ in near], [role() for _ in range(3)]
    for r, (d, e) in zip(r_az, near):
        block = gp.at[y, zl, c]
        send(r, block, block, seq_of(y, (zl + d) % 4, oc if e else c), g)
    wait(r_w[0][4], wt.at[:, :, oc])
    hid[...] = sb[...].astype(F32) + out_part(x)
    hid[...] += out_part(xm)
    hid[...] += out_part(xp)
    wait(r_mx[2], at.at[x2, 0, 0:3])
    wait(r_mx[3], at.at[x2, 1, 0:3])
    hid[...] += out_part(x2)
    spread(hid, KC, gain, fw, pm, rm, r_pm)
    flush(sent_d)

    @pl.when(jnp.logical_not(same))
    def _():
        for r, (src, there, _) in zip(r_perm, moved):
            copy(r, src, there, part_s, part_g).wait_send()

    for r, (d, e) in zip(r_az, near):
        wait(r, gp.at[y, (zl + 4 - d) % 4, oc if e else c])
    for d in (1, 2, 3):
        send(r_ay[d - 1], gp.at[y], gp.at[y], seq_of((y + d) % 4, zl, c), g)
    main_pred = combine(KC, rm, r_pm)
    for d in (1, 2, 3):
        wait(r_ay[d - 1], gp.at[(y + 4 - d) % 4])

    lane = lax.broadcasted_iota(jnp.int32, (8, 128), 1)
    pieces = []
    for yy in range(4):
        for zz in range(4):
            a0, a1 = gp[yy, zz, 0, :, 0:128], gp[yy, zz, 0, :, 128:192]
            b0, b1 = gp[yy, zz, 1, :, 0:64], gp[yy, zz, 1, :, 64:192]
            pieces += [a0, jnp.concatenate([a1, b0], axis=1), b1]
    slots = jnp.concatenate(pieces, axis=1)
    upper = slots.astype(BF16)
    lower = (slots - upper.astype(F32)).astype(BF16)
    both = jnp.concatenate([upper, lower], axis=0)
    picked = lax.dot_general(both, hot[...], NT, preferred_element_type=F32)
    picked = picked[0:8] + picked[8:16]

    first = s * ROWS
    frame = first // FRAME_TOK
    last = (first + ROWS - 1) // FRAME_TOK
    owned = first + lax.broadcasted_iota(jnp.int32, (8, ROWS), 1)
    strength = 1.0 + jnp.where(owned // FRAME_TOK == frame, flags[frame], flags[last]).astype(F32)
    outb[g] = picked + strength * (main_pred - picked)
    for d in range(1, 8):
        send(r_out[d - 1], outb.at[g], outb.at[g], s, (g + d) % 8)
    flush(len(started) - 7)
    for d in range(1, 8):
        wait(r_out[d - 1], outb.at[(g + 8 - d) % 8])
    for i in range(8):
        out[i * 8 : (i + 1) * 8, :] = outb[i]

    flush(len(started))


def per_device(
    stream, normed, qkv_weight, out_weight, final_gain, final_weight, guide_stream, guide_normed,
    guide_qkv, guide_out, guide_gain, guide_final, layout, flags,
):
    anyw = pl.BlockSpec(memory_space=pl.ANY)
    vmem = pl.BlockSpec(memory_space=pltpu.VMEM)
    smem = pl.BlockSpec(memory_space=pltpu.SMEM)
    v = pltpu.VMEM
    scratch = [
        v((8, ROWS, KC), BF16),
        v((8, ROWS, GKC), BF16),
        v((3, 5120, 384), BF16),
        v((3, 4, 4, 2, 64, HD), BF16),
        v((4, 4, 2, 160, 384), BF16),
        v((4, 4, 2, 64, HD), BF16),
        v((2, 2, 160, 64), BF16),
        v((2, 2, 64, 64), BF16),
        v((ROWS, KC), BF16),
        v((ROWS, GKC), BF16),
        v((3, ROWS, 384), F32),
        v((3, ROWS, HD), F32),
        v((3, 4, ROWS, HD), BF16),
        v((4, ROWS, HD), BF16),
        v((2, 4, 2, 4, ROWS, HD), BF16),
        v((1, 4 * ROWS), F32),
        v((1, 4 * ROWS), F32),
        v((HD, 4 * ROWS), F32),
        v((4 * ROWS, HD), BF16),
        v((4, 2, 4, ROWS, HD), BF16),
        v((ROWS, TOKENS), BF16),
        v((ROWS, KC), F32),
        v((ROWS, GKC), F32),
        v((160, 64), BF16),
        v((8, 16, 256), F32),
        v((8, 16, 256), F32),
        v((8, 16, 256), F32),
        v((8, 16, 256), F32),
        v((4, 4, 2, 8, ROWS), F32),
        v((8, 8, ROWS), F32),
        pltpu.SemaphoreType.DMA((192,)),
        pltpu.SemaphoreType.DMA((192,)),
        pltpu.SemaphoreType.DMA((8,)),
    ]
    guided = pl.pallas_call(
        body,
        out_shape=jax.ShapeDtypeStruct((64, ROWS), F32),
        in_specs=[anyw] * 4 + [vmem, vmem] + [anyw] * 4 + [vmem, anyw, vmem, smem],
        out_specs=vmem,
        scratch_shapes=scratch,
        compiler_params=pltpu.CompilerParams(
            collective_id=0, has_side_effects=True, vmem_limit_bytes=56 * 1024 * 1024
        ),
        cost_estimate=pl.CostEstimate(
            flops=6_000_000_000, bytes_accessed=20_000_000, transcendentals=5_000_000
        ),
    )(
        stream, normed, jnp.transpose(qkv_weight, (1, 0, 2)), out_weight.T,
        final_gain.reshape(40, 128), final_weight.T, guide_stream, guide_normed,
        jnp.transpose(guide_qkv, (1, 0, 2)), guide_out.T, guide_gain.reshape(16, 128), guide_final,
        layout.reshape(48, 128), flags,
    )
    return guided.T


def solution(mesh):
    placed = (
        P("seq", "head"),
        P("seq", "head"),
        P(None, None, "head"),
        P("head", "seq"),
        P(),
        P("seq", None),
        P("seq", "head"),
        P("seq", "head"),
        P("seq", None, "head"),
        P("head", "seq"),
        P(),
        P("seq", None),
        P(),
        P(),
    )
    return jax.shard_map(
        per_device, mesh=mesh, in_specs=placed, out_specs=P("seq", None), check_vma=False
    )
```
